256 devices in a mesh: dp: 32 (over x, y, core), expert: 8 (over z).
Axes of the slice: x: 4, y: 4, z: 8, core: 2. Of those that a mesh axis runs over, the one named last changes fastest.
Arguments:
- hidden_rows: bfloat16 [32768, 6, 1536], P(('dp', 'expert')), may hold values from -6 to 6
- out_grads: bfloat16 [32768, 2560], P(('dp', 'expert')), may hold values from -12 to 12
- gates: float32 [32768, 6], P(('dp', 'expert')), may hold values from 0.1 to 1
- routes: int32 [32768, 6], P(('dp', 'expert')), may hold values from 0 to 159, all different within a row; in each aligned block of 128 rows (0 to 127, 128 to 255, ...) at most 6 rows name the same one
- panel_a: float32 [256, 32, 384], P(('dp', 'expert')), may hold values from -6 to 6
- panel_g: float32 [256, 32, 640], P(('dp', 'expert')), may hold values from -6 to 6
Outputs:
- input_cov: float32 [256, 384, 1536], P(('dp', 'expert'))
- grad_cov: float32 [256, 640, 2560], P(('dp', 'expert'))
- input_panel: float32 [256, 32, 384], P(('dp', 'expert'))
- grad_panel: float32 [256, 32, 640], P(('dp', 'expert'))
The draws below stay inside these ranges and needn't reach their ends.
Inputs may be any that keep to these rules, and one draw needn't show every extreme that they name: `routes`: each row names 6 different experts. Among the 128 rows of one device no expert is named more than 6 times, a bound that some block reaches.
All inputs are finite; a program needn't handle non-finite values.
Results may differ from the reference program's by a relative error of at most 0.0037.
Values may be sent and summed in bfloat16 or wider, within the bound.
No kernel may reach another device: no remote copies, remote signals or barrier semaphores. Data moves between devices by JAX's collectives and lax.ppermute only.
A program may use at most 128 MiB of HBM per device.

```python
import math
import jax
import jax.numpy as jnp
import numpy as np
from jax import lax

FF = 1536
DW = 2560
ROUTED = 160
TOP = 6
PW = 32
OWNERS = 4
TOK_DEV = 128
TOKENS = 32768
FLIGHT = 64
CAP = 6
N_DP = 32
N_EXPERT = 8


def level_of(stream_key, extent, split, low, largest):
    def one(dim, parts):
        draws = jax.random.uniform(jax.random.fold_in(jax.random.fold_in(stream_key, 6), dim), (parts,), jnp.float32, low / len(split), largest / len(split))
        return jnp.repeat(jnp.exp(draws), extent[dim] // parts).reshape((-1,) + (1,) * (len(extent) - dim - 1))

    loudness = one(*split[0])
    for cut in split[1:]:
        loudness = loudness * one(*cut)
    return loudness


def routed_block(own_key, own, number, rows, amount, top, bound, lean):
    ranking = jax.random.permutation(own_key, amount)
    crowded, usual = portions_of(amount, rows * top, bound, lean, True), portions_of(amount, rows * top, bound, lean, False)
    places = jnp.arange(amount)

    def named(sizes, offset_by):
        used = int((sizes > 0).sum())
        fixed = max(1, used // 4)
        shifted = fixed + (places - fixed + offset_by * (used - fixed)) % max(1, amount - fixed)
        return jnp.zeros((amount,), jnp.int32).at[ranking[jnp.where(places < fixed, places, shifted)]].set(jnp.asarray(sizes, jnp.int32))

    sizes = jnp.where(number % 4 == 0, named(crowded, number // 4), named(usual, number - number // 4 - 1))
    mixed = jax.random.permutation(jax.random.fold_in(own, 3), amount)
    donor, sink = mixed[0:amount // 2 * 2:2], mixed[1:amount // 2 * 2:2]
    margin = jnp.minimum(sizes[donor] - 1, bound - sizes[sink]) // 2
    margin = jnp.where((donor == ranking[0]) | (sink == ranking[0]) | (sizes[sink] == 0), 0, jnp.maximum(margin, 0))
    shifted = jax.random.randint(jax.random.fold_in(own, 4), (amount // 2,), 0, 1 << 20) % (margin + 1)
    sizes = sizes.at[donor].add(-shifted).at[sink].add(shifted)
    members = jnp.searchsorted(jnp.cumsum(sizes), jnp.arange(rows * top), side="right").astype(jnp.int32)
    table = members.reshape(top, rows).T
    table = table[jax.random.permutation(jax.random.fold_in(own, 1), rows)]
    offset_by = jax.random.randint(jax.random.fold_in(own, 2), (rows, 1), 0, top)
    return jnp.take_along_axis(table, (jnp.arange(top)[None, :] + offset_by) % top, axis=1)


def portions_of(count, total, most, skew, full):
    loads = [(1 << 20) // math.isqrt(rank ** skew) + 1 for rank in range(1, count + 1)]
    largest = most if full else min(most, max(-(-total // count), total * loads[0] // sum(loads)))
    least = 1 if total - largest >= count - 1 else 0
    given, surplus = [largest] + [least] * (count - 1), total - largest - least * (count - 1)
    while surplus > 0:
        movable = [i for i in range(1, count) if given[i] < largest] or [i for i in range(1, count) if given[i] < most]
        whole, remaining = sum([loads[i] for i in movable]), surplus
        for i in movable:
            more = min(most - given[i], max(1, remaining * loads[i] // whole), surplus)
            given[i] = given[i] + more
            surplus = surplus - more
    return np.array(given)


def gaussian(stream_key, extent, spread, reach, shards=(), kind=jnp.bfloat16):
    level = level_of(stream_key, extent, shards, -0.22, 0.18) if shards else 1.0
    drawn = jax.random.normal(stream_key, extent, jnp.float32) * spread * level
    return jnp.minimum(jnp.maximum(drawn, -reach), reach).astype(kind)


def setup_inputs(seed: int = 0) -> dict:
    arg_keys = jax.random.split(jax.random.key(seed), 7)
    hidden_rows = gaussian(arg_keys[0], (TOKENS, TOP, FF), 1.0, 6.0, ((0, 256),))
    out_grads = gaussian(arg_keys[1], (TOKENS, DW), 2.0, 12.0, ((0, 256),))
    gates = jnp.clip(jnp.exp(math.log(1.0) - 2.3025851 * jax.random.uniform(arg_keys[2], (TOKENS, TOP), jnp.float32) ** level_of(arg_keys[2], (TOKENS, TOP), ((0, 256),), -0.2, 0.2)), 0.1, 1.0)
    routes_keys = jax.random.split(jax.random.fold_in(arg_keys[3], 1), TOKENS // TOK_DEV)
    routes_turns = jax.random.permutation(jax.random.fold_in(arg_keys[3], 3), TOKENS // TOK_DEV)
    routes = jax.vmap(lambda own, number: routed_block(jax.random.fold_in(arg_keys[3], 2), own, number, TOK_DEV, ROUTED, TOP, CAP, 1))(routes_keys, routes_turns).reshape((TOKENS, TOP))
    panel_a = gaussian(arg_keys[4], (OWNERS * FLIGHT, PW, FF // OWNERS), 1.0, 6.0, ((0, 256),), jnp.float32)
    panel_g = gaussian(arg_keys[5], (OWNERS * FLIGHT, PW, DW // OWNERS), 1.0, 6.0, ((0, 256),), jnp.float32)
    return dict(hidden_rows=hidden_rows, out_grads=out_grads, gates=gates, routes=routes, panel_a=panel_a, panel_g=panel_g)


def reference(hidden_rows, out_grads, gates, routes, panel_a, panel_g):
    entries = TOKENS * TOP
    groups = FLIGHT // N_EXPERT
    expert_ids = routes.reshape(entries).astype(jnp.int32)
    sorted_pos = jnp.argsort(expert_ids, stable=True).astype(jnp.int32)
    window = jnp.arange(FLIGHT, dtype=jnp.int32)
    counts = jnp.sum((expert_ids[:, None] == window[None, :]).astype(jnp.int32), axis=0)
    starts = jnp.cumsum(counts) - counts
    longest = N_DP * N_EXPERT * CAP
    flat_hidden = hidden_rows.reshape(entries, FF)
    flat_gates = gates.reshape(entries)
    norm_factor = ROUTED / (TOKENS * TOP)
    full_a = panel_a.reshape(groups, OWNERS, N_EXPERT, PW, FF // OWNERS).transpose(0, 2, 1, 3, 4)
    full_a = full_a.reshape(FLIGHT, OWNERS, PW, FF // OWNERS)
    full_g = panel_g.reshape(groups, OWNERS, N_EXPERT, PW, DW // OWNERS).transpose(0, 2, 1, 3, 4)
    full_g = full_g.reshape(FLIGHT, OWNERS, PW, DW // OWNERS)

    def per_expert(expert):
        offsets = jnp.arange(longest, dtype=jnp.int32)
        clipped = jnp.minimum(starts[expert] + offsets, entries - 1).astype(jnp.int32)
        picked = sorted_pos[clipped]
        usable = offsets < counts[expert]
        hidden_part = jnp.where(usable[:, None], flat_hidden[picked], jnp.zeros((), jnp.bfloat16)).astype(jnp.float32)
        token_pos = picked // TOP
        grad_full = flat_gates[picked][:, None] * out_grads[token_pos].astype(jnp.float32)
        grad_part = lax.optimization_barrier(grad_full.astype(jnp.bfloat16)).astype(jnp.float32)
        grad_part = jnp.where(usable[:, None], grad_part, jnp.zeros((), jnp.float32))
        cov_in = jnp.dot(hidden_part.T, hidden_part, precision=lax.Precision.HIGHEST) * norm_factor
        cov_grad = jnp.dot(grad_part.T, grad_part, precision=lax.Precision.HIGHEST) * norm_factor
        panel_in = full_a[expert].transpose(1, 0, 2).reshape(PW, FF)
        panel_out = full_g[expert].transpose(1, 0, 2).reshape(PW, DW)
        rot_in = jnp.dot(panel_in, cov_in, precision=lax.Precision.HIGHEST)
        rot_out = jnp.dot(panel_out, cov_grad, precision=lax.Precision.HIGHEST)
        rot_in = rot_in.reshape(PW, OWNERS, FF // OWNERS).transpose(1, 0, 2)
        rot_out = rot_out.reshape(PW, OWNERS, DW // OWNERS).transpose(1, 0, 2)
        return (cov_in.reshape(OWNERS, FF // OWNERS, FF), cov_grad.reshape(OWNERS, DW // OWNERS, DW), rot_in, rot_out)

    stats_in, stats_out, rots_in, rots_out = lax.map(per_expert, window)

    def arrange(stacked):
        tail = stacked.shape[2:]
        shaped = stacked.reshape((groups, N_EXPERT, OWNERS) + tail)
        shaped = shaped.transpose((0, 2, 1) + tuple(range(3, 3 + len(tail))))
        return shaped.reshape((FLIGHT * OWNERS,) + tail)

    return (arrange(stats_in), arrange(stats_out), arrange(rots_in), arrange(rots_out))
```

```python
import functools

import jax
import jax.numpy as jnp
from jax import lax
from jax.experimental import pallas as pl
from jax.experimental.pallas import tpu as pltpu
from jax.sharding import Mesh
from jax.sharding import PartitionSpec as P

ROUTED = 160
OWNERS = 4
CAP = 6
GROUPS = 8
Z = 8
FLIGHT = GROUPS * Z
AXES = ("x", "yh", "yl", "core", "z")
GRAD_CHUNKS = ((0, 2), (2, 6))
HIDDEN_CHUNKS = ((0, 6),)
f32 = jnp.float32
bf16 = jnp.bfloat16


def params(mib):
    return pltpu.CompilerParams(vmem_limit_bytes=mib * 2**20)


VMEM = pl.BlockSpec(memory_space=pltpu.VMEM)
SMEM = pl.BlockSpec(memory_space=pltpu.SMEM)


def slot_table(routes_ref, slots, tok):
    ids = routes_ref[...]
    upper = (
        lax.broadcasted_iota(jnp.int32, (tok, tok), 0) < lax.broadcasted_iota(jnp.int32, (tok, tok), 1)
    ).astype(bf16)
    window = lax.broadcasted_iota(jnp.int32, (FLIGHT, tok), 0)
    seen = jnp.zeros((FLIGHT, 1), f32)
    out = []
    for k in range(slots):
        named = (window == ids[k : k + 1, :]).astype(f32)
        before = jnp.dot(named.astype(bf16), upper, preferred_element_type=f32) + seen
        slot = jnp.sum(named * before, axis=0, keepdims=True)
        seen = seen + jnp.sum(named, axis=1, keepdims=True)
        out.append((ids[k : k + 1, :], slot.astype(jnp.int32)))
    return out


def targets(table, my_z, first, last):
    width = last - first
    out = []
    for ids, slot in table:
        away = (ids - my_z) & (Z - 1)
        group = lax.shift_right_logical(ids, 3)
        place = away * (GROUPS * width) + group * width + slot - first
        ok = (ids < FLIGHT) & (slot >= first) & (slot < last)
        out.append(jnp.where(ok, place, -1))
    return out


def pack_grad_kernel(chunks, z_ref, routes_ref, gates_ref, grads_ref, *outs):
    slots, tok = routes_ref.shape
    table = slot_table(routes_ref, slots, tok)
    for number, (first, last) in enumerate(chunks):
        rows = FLIGHT * (last - first)
        block = GROUPS * (last - first)
        position = lax.broadcasted_iota(jnp.int32, (rows, tok), 0)
        pick = jnp.zeros((rows, tok), f32)
        weight = jnp.zeros((rows, tok), f32)
        for k, target in enumerate(targets(table, z_ref[0, 0], first, last)):
            hit = position == target
            pick = jnp.where(hit, 1.0, pick)
            weight = jnp.where(hit, gates_ref[k : k + 1, :], weight)
        gate = jnp.sum(weight, axis=1, keepdims=True)
        picked = jnp.dot(pick.astype(bf16), grads_ref[...], preferred_element_type=f32)
        scaled = gate * picked
        for away in range(Z):
            outs[number * Z + away][...] = scaled[away * block : (away + 1) * block, :].astype(bf16)


def pack_hidden_kernel(chunks, z_ref, routes_ref, hidden_ref, *outs):
    slots, tok = routes_ref.shape
    table = slot_table(routes_ref, slots, tok)
    for number, (first, last) in enumerate(chunks):
        rows = FLIGHT * (last - first)
        block = GROUPS * (last - first)
        position = lax.broadcasted_iota(jnp.int32, (rows, tok), 0)
        picked = None
        for k, target in enumerate(targets(table, z_ref[0, 0], first, last)):
            hit = (position == target).astype(f32).astype(bf16)
            part = jnp.dot(hit, hidden_ref[k], preferred_element_type=f32)
            picked = part if picked is None else picked + part
        for away in range(Z):
            outs[number * Z + away][...] = picked[away * block : (away + 1) * block, :].astype(bf16)


def packed_shapes(chunks, features):
    return [
        jax.ShapeDtypeStruct((GROUPS * (last - first), features), bf16)
        for first, last in chunks
        for _ in range(Z)
    ]


def arrange_kernel(width, *refs):
    ins, out_ref, held = refs[:Z], refs[Z], refs[Z + 1]
    block = GROUPS * width
    rows = Z * block
    for away in range(Z):
        held[away * block : (away + 1) * block, :] = ins[away][...]
    source = lax.broadcasted_iota(jnp.int32, (1, rows), 1)
    away = source // block
    rest = source - away * block
    group = rest // width
    slot = rest - group * width
    place = group * (Z * width) + away * width + slot
    order = (lax.broadcasted_iota(jnp.int32, (rows, rows), 0) == place).astype(f32).astype(bf16)
    moved = jnp.dot(order, held[...], preferred_element_type=f32)
    for group in range(GROUPS):
        piece = moved[group * block : (group + 1) * block, :].astype(bf16)
        out_ref[2 * group] = piece
        out_ref[2 * group + 1] = piece


def arrange(pieces, width):
    block, features = pieces[0].shape
    return pl.pallas_call(
        functools.partial(arrange_kernel, width),
        out_shape=jax.ShapeDtypeStruct((2 * GROUPS, block, features), bf16),
        in_specs=[VMEM] * Z,
        out_specs=VMEM,
        scratch_shapes=[pltpu.VMEM((Z * block, features), bf16)],
        compiler_params=params(32),
        cost_estimate=pl.CostEstimate(
            flops=2 * (Z * block) ** 2 * features, bytes_accessed=6 * Z * block * features, transcendentals=0
        ),
    )(*pieces)


def thirds(value):
    high = value.astype(bf16)
    rest = value - high.astype(f32)
    middle = rest.astype(bf16)
    low = (rest - middle.astype(f32)).astype(bf16)
    return jnp.concatenate([high, middle, low], axis=0)


def added(value, rows):
    return value[:rows] + value[rows : 2 * rows] + value[2 * rows :]


def stats_kernel(norm, tile, count, q_ref, panel_ref, *refs):
    rows, (cov_ref, out_ref), turned = refs[:count], refs[count : count + 2], refs[count + 2 :]
    block = cov_ref.shape[0]
    features = cov_ref.shape[1]
    panel_rows = out_ref.shape[0]
    own = pl.ds(pl.multiple_of(q_ref[0, 0] * block, 128), block)
    for row, turn in zip(rows, turned):
        turn[...] = row[:, own].T
    for start in range(0, features, tile):
        total = None
        for row, turn in zip(rows, turned):
            part = jnp.dot(turn[...], row[:, start : start + tile], preferred_element_type=f32)
            total = part if total is None else total + part
        cov_ref[:, start : start + tile] = total * norm
    pieces = [thirds(panel_ref[quarter]) for quarter in range(OWNERS)]
    result = jnp.zeros(out_ref.shape, f32)
    for row in rows:
        share = jnp.zeros((3 * panel_rows, row.shape[0]), f32)
        for quarter in range(OWNERS):
            share = share + lax.dot_general(
                pieces[quarter],
                row[:, quarter * block : (quarter + 1) * block],
                (((1,), (1,)), ((), ())),
                preferred_element_type=f32,
            )
        turned_panel = thirds(added(share, panel_rows))
        result = result + added(jnp.dot(turned_panel, row[:, own], preferred_element_type=f32), panel_rows)
    out_ref[...] = result * norm


def stats(quarter, panel, rows, norm, tile):
    features = rows[0].shape[1]
    block = features // OWNERS
    total = sum(row.shape[0] for row in rows)
    return pl.pallas_call(
        functools.partial(stats_kernel, norm, tile, len(rows)),
        out_shape=(
            jax.ShapeDtypeStruct((block, features), f32),
            jax.ShapeDtypeStruct((panel.shape[1], block), f32),
        ),
        in_specs=[SMEM, VMEM] + [VMEM] * len(rows),
        out_specs=(VMEM, VMEM),
        scratch_shapes=[pltpu.VMEM((block, row.shape[0]), bf16) for row in rows],
        compiler_params=params(48),
        cost_estimate=pl.CostEstimate(
            flops=2 * total * features * block,
            bytes_accessed=2 * total * features + 4 * features * block,
            transcendentals=0,
        ),
    )(quarter, panel, *rows)


def through_z(pieces):
    out = [pieces[0]]
    for away in range(1, Z):
        out.append(lax.ppermute(pieces[away], "z", [(i, (i + away) % Z) for i in range(Z)]))
    return out


def through_xy(pieces, width):
    placed = arrange(pieces, width)
    mine = lax.all_to_all(placed, ("x", "yh", "yl"), 0, 0, tiled=True)
    mine = mine.reshape(-1, mine.shape[-1])
    other = lax.ppermute(mine, "core", [(0, 1), (1, 0)])
    return mine, other


def per_device(hidden_rows, out_grads, gates, routes, panel_a, panel_g):
    tok, slots, width_in = hidden_rows.shape
    width_out = out_grads.shape[1]
    norm = ROUTED / (tok * 256 * slots)
    routes_t = routes.T
    my_z = lax.axis_index("z").astype(jnp.int32).reshape(1, 1)
    quarter = (lax.axis_index("yl") * 2 + lax.axis_index("core")).astype(jnp.int32).reshape(1, 1)
    packed_g = pl.pallas_call(
        functools.partial(pack_grad_kernel, GRAD_CHUNKS),
        out_shape=packed_shapes(GRAD_CHUNKS, width_out),
        in_specs=[SMEM, VMEM, VMEM, VMEM],
        out_specs=[VMEM] * (Z * len(GRAD_CHUNKS)),
        compiler_params=params(32),
    )(my_z, routes_t, gates.T, out_grads)
    packed_h = pl.pallas_call(
        functools.partial(pack_hidden_kernel, HIDDEN_CHUNKS),
        out_shape=packed_shapes(HIDDEN_CHUNKS, width_in),
        in_specs=[SMEM, VMEM, VMEM],
        out_specs=[VMEM] * (Z * len(HIDDEN_CHUNKS)),
        compiler_params=params(32),
    )(my_z, routes_t, hidden_rows.transpose(1, 0, 2))
    chunks = [
        (list(packed_g[n * Z : (n + 1) * Z]), last - first) for n, (first, last) in enumerate(GRAD_CHUNKS)
    ] + [(list(packed_h[n * Z : (n + 1) * Z]), last - first) for n, (first, last) in enumerate(HIDDEN_CHUNKS)]
    full_a = lax.all_gather(panel_a[0], ("yl", "core"), axis=0)
    full_g = lax.all_gather(panel_g[0], ("yl", "core"), axis=0)
    arrived = []
    for number, (pieces, width) in enumerate(chunks):
        got = through_z(pieces)
        if number + 1 < len(chunks):
            got, later = lax.optimization_barrier((got, chunks[number + 1][0]))
            chunks[number + 1] = (list(later), chunks[number + 1][1])
        arrived.append(through_xy(got, width))
    rows_g = [part for pair in arrived[: len(GRAD_CHUNKS)] for part in pair]
    rows_h = [part for pair in arrived[len(GRAD_CHUNKS) :] for part in pair]
    grad_cov, grad_panel = stats(quarter, full_g, rows_g, norm, 512)
    input_cov, input_panel = stats(quarter, full_a, rows_h, norm, 512)
    return (input_cov[None], grad_cov[None], input_panel[None], grad_panel[None])


def solution(mesh):
    split = Mesh(mesh.devices.reshape(4, 2, 2, 2, Z), AXES)
    return jax.shard_map(
        per_device,
        mesh=split,
        in_specs=(
            P(AXES, None, None),
            P(AXES, None),
            P(AXES, None),
            P(AXES, None),
            P(AXES, None, None),
            P(AXES, None, None),
        ),
        out_specs=(P(AXES, None, None),) * 4,
        check_vma=False,
    )
```

```python
import functools

import jax
import jax.numpy as jnp
from jax import lax
from jax.experimental import pallas as pl
from jax.experimental.pallas import tpu as pltpu
from jax.sharding import Mesh
from jax.sharding import PartitionSpec as P

ROUTED = 160
OWNERS = 4
Z = 8
DESTS = 32
FLIGHT = 64
AXES = ("x", "yh", "yl", "core", "z")
SPLITS = {2: (4, 1), 4: (2, 2), 6: (4, 2)}
GRAD_CHUNKS = ((0, 4), (4, 6))
HIDDEN_CHUNKS = ((0, 6),)
f32 = jnp.float32
bf16 = jnp.bfloat16
VMEM = pl.BlockSpec(memory_space=pltpu.VMEM)
SMEM = pl.BlockSpec(memory_space=pltpu.SMEM)
ANY = pl.BlockSpec(memory_space=pl.ANY)


def params(mib):
    return pltpu.CompilerParams(vmem_limit_bytes=mib * 2**20)


def one_hot(rows, target):
    position = lax.broadcasted_iota(jnp.int32, (rows, target.shape[1]), 0)
    return (position == target).astype(f32).astype(bf16)


def slot_table(routes_ref):
    slots, tok = routes_ref.shape
    ids = routes_ref[...]
    upper = (
        lax.broadcasted_iota(jnp.int32, (tok, tok), 0) < lax.broadcasted_iota(jnp.int32, (tok, tok), 1)
    ).astype(f32).astype(bf16)
    window = lax.broadcasted_iota(jnp.int32, (FLIGHT, tok), 0)
    seen = jnp.zeros((FLIGHT, 1), f32)
    out = []
    for k in range(slots):
        named = (window == ids[k : k + 1, :]).astype(f32)
        before = jnp.dot(named.astype(bf16), upper, preferred_element_type=f32) + seen
        slot = jnp.sum(named * before, axis=0, keepdims=True)
        seen = seen + jnp.sum(named, axis=1, keepdims=True)
        out.append((ids[k : k + 1, :], slot.astype(jnp.int32)))
    return out


def targets(table, my_half, first, last):
    width = last - first
    out = []
    for ids, slot in table:
        dest = lax.shift_right_logical(ids, 4) * Z + (ids & (Z - 1))
        across = (lax.shift_right_logical(ids, 3) & 1) ^ my_half
        place = dest * (2 * width) + across * width + slot - first
        ok = (ids < FLIGHT) & (slot >= first) & (slot < last)
        out.append(jnp.where(ok, place, -1))
    return out


def spread(compact, width, out_ref):
    cuts, groups = SPLITS[width]
    block = cuts * 2 * width
    per = DESTS // groups
    lanes = out_ref.shape[2]
    source = lax.broadcasted_iota(jnp.int32, (1, per * 2 * width), 1)
    dest = lax.div(source, 2 * width)
    start = dest * block + source - dest * (2 * width)
    moves = [one_hot(per * block, start + cut * 2 * width) for cut in range(cuts)]
    for group in range(groups):
        total = None
        for cut, move in enumerate(moves):
            piece = compact[group * per * 2 * width : (group + 1) * per * 2 * width, cut * lanes : (cut + 1) * lanes]
            part = jnp.dot(move, piece, preferred_element_type=f32)
            total = part if total is None else total + part
        out_ref[group * per : (group + 1) * per] = total.astype(bf16).reshape(per, block, lanes)


def pack_grad_kernel(half_ref, routes_ref, gates_ref, grads_ref, *outs):
    tok = routes_ref.shape[1]
    table = slot_table(routes_ref)
    for (first, last), out_ref in zip(GRAD_CHUNKS, outs):
        rows = FLIGHT * (last - first)
        position = lax.broadcasted_iota(jnp.int32, (rows, tok), 0)
        pick = jnp.zeros((rows, tok), f32)
        weight = jnp.zeros((rows, tok), f32)
        for k, target in enumerate(targets(table, half_ref[0, 0], first, last)):
            hit = position == target
            pick = jnp.where(hit, 1.0, pick)
            weight = jnp.where(hit, gates_ref[k : k + 1, :], weight)
        gate = jnp.sum(weight, axis=1, keepdims=True)
        picked = jnp.dot(pick.astype(bf16), grads_ref[...], preferred_element_type=f32)
        spread((gate * picked).astype(bf16), last - first, out_ref)


def pack_hidden_kernel(half_ref, routes_ref, hidden_ref, *outs):
    table = slot_table(routes_ref)
    for (first, last), out_ref in zip(HIDDEN_CHUNKS, outs):
        rows = FLIGHT * (last - first)
        picked = None
        for k, target in enumerate(targets(table, half_ref[0, 0], first, last)):
            part = jnp.dot(one_hot(rows, target), hidden_ref[k], preferred_element_type=f32)
            picked = part if picked is None else picked + part
        spread(picked.astype(bf16), last - first, out_ref)


def packed_shapes(chunks, features):
    out = []
    for first, last in chunks:
        cuts = SPLITS[last - first][0]
        out.append(jax.ShapeDtypeStruct((DESTS, cuts * 2 * (last - first), features // cuts), bf16))
    return out


def gather_kernel(width, in_ref, own_ref, across_ref):
    cuts, groups = SPLITS[width]
    block = cuts * 2 * width
    per = DESTS // groups
    lanes = in_ref.shape[2]
    source = lax.broadcasted_iota(jnp.int32, (1, per * block), 1)
    sender = lax.div(source, block)
    rest = source - sender * block
    cut_of = lax.div(rest, 2 * width)
    rest = rest - cut_of * (2 * width)
    half = lax.div(rest, width)
    place = half * (per * width) + sender * width + rest - half * width
    moves = [one_hot(2 * per * width, jnp.where(cut_of == cut, place, -1)) for cut in range(cuts)]
    for group in range(groups):
        piece = in_ref[group * per : (group + 1) * per].reshape(per * block, lanes)
        for cut, move in enumerate(moves):
            moved = jnp.dot(move, piece, preferred_element_type=f32).astype(bf16)
            here = slice(group * per * width, (group + 1) * per * width)
            there = slice(cut * lanes, (cut + 1) * lanes)
            own_ref[here, there] = moved[: per * width]
            across_ref[here, there] = moved[per * width :]


def gathered(arrived, width, features):
    rows = DESTS * width
    return pl.pallas_call(
        functools.partial(gather_kernel, width),
        out_shape=(jax.ShapeDtypeStruct((rows, features), bf16),) * 2,
        in_specs=[VMEM],
        out_specs=(VMEM, VMEM),
        compiler_params=params(32),
        cost_estimate=pl.CostEstimate(
            flops=4 * rows * rows * features, bytes_accessed=8 * rows * features, transcendentals=0
        ),
    )(arrived)


def thirds(value):
    high = value.astype(bf16)
    rest = value - high.astype(f32)
    middle = rest.astype(bf16)
    low = (rest - middle.astype(f32)).astype(bf16)
    return jnp.concatenate([high, middle, low], axis=0)


def added(value, rows):
    return value[:rows] + value[rows : 2 * rows] + value[2 * rows :]


def stats_kernel(norm, offset, count, q_ref, *refs):
    panels, rows = refs[:OWNERS], refs[OWNERS : OWNERS + count]
    cov_ref, out_ref, held, turned, sems = refs[OWNERS + count :]
    block, tile = cov_ref.shape
    panel_rows = out_ref.shape[0]
    step = pl.program_id(0)
    quarter = q_ref[0, 0]

    def columns(away):
        return pl.ds(pl.multiple_of((quarter ^ away) * block, 128), block)

    @pl.when(step == 0)
    def _():
        copies = []
        at = 0
        for number, row in enumerate(rows):
            size = row.shape[0]
            copy = pltpu.make_async_copy(row, held.at[at : at + size, :], sems.at[number])
            copy.start()
            copies.append((copy, at, size))
            at += size
        for copy, at, size in copies:
            copy.wait()
        turned[...] = held[:, columns(0)].T

    tile_at = pl.ds(pl.multiple_of(step * tile, 128), tile)
    cov_ref[...] = jnp.dot(turned[...], held[:, tile_at], preferred_element_type=f32) * norm

    @pl.when(step == pl.num_programs(0) - 1)
    def _():
        share = None
        for away in range(OWNERS):
            part = lax.dot_general(
                thirds(panels[away][:, offset : offset + block]),
                held[:, columns(away)],
                (((1,), (1,)), ((), ())),
                preferred_element_type=f32,
            )
            share = part if share is None else share + part
        product = jnp.dot(thirds(added(share, panel_rows)), held[:, columns(0)], preferred_element_type=f32)
        out_ref[...] = added(product, panel_rows) * norm


def stats(quarter, panels, offset, rows, norm, tile):
    features = rows[0].shape[1]
    block = features // OWNERS
    total = sum(row.shape[0] for row in rows)
    panel_rows, panel_width = panels[0].shape
    return pl.pallas_call(
        functools.partial(stats_kernel, norm, offset, len(rows)),
        grid=(features // tile,),
        out_shape=(
            jax.ShapeDtypeStruct((block, features), f32),
            jax.ShapeDtypeStruct((panel_rows, block), f32),
        ),
        in_specs=[SMEM] + [pl.BlockSpec((panel_rows, panel_width), lambda n: (0, 0))] * OWNERS + [ANY] * len(rows),
        out_specs=(
            pl.BlockSpec((block, tile), lambda n: (0, n)),
            pl.BlockSpec((panel_rows, block), lambda n: (0, 0)),
        ),
        scratch_shapes=[
            pltpu.VMEM((total, features), bf16),
            pltpu.VMEM((block, total), bf16),
            pltpu.SemaphoreType.DMA((len(rows),)),
        ],
        compiler_params=params(40),
        cost_estimate=pl.CostEstimate(
            flops=2 * total * features * block,
            bytes_accessed=2 * total * features + 4 * features * block,
            transcendentals=0,
        ),
    )(quarter, *panels, *rows)


def core_swapped(value):
    return lax.ppermute(value, "core", [(0, 1), (1, 0)])


def y_moved(value, flip):
    return lax.ppermute(value, ("yh", "yl"), [(i, i ^ flip) for i in range(4)])


def along_y(own, across):
    pieces = [own, y_moved(own, 1), y_moved(across, 3), y_moved(across, 2)]
    return pieces + [core_swapped(piece) for piece in pieces]


def per_device(hidden_rows, out_grads, gates, routes, panel_a, panel_g):
    tok, slots, width_in = hidden_rows.shape
    width_out = out_grads.shape[1]
    norm = ROUTED / (tok * 256 * slots)
    routes_t = routes.T
    my_half = lax.axis_index("yh").astype(jnp.int32).reshape(1, 1)
    quarter = (lax.axis_index("yl") * 2 + lax.axis_index("core")).astype(jnp.int32).reshape(1, 1)
    packed_h = pl.pallas_call(
        pack_hidden_kernel,
        out_shape=packed_shapes(HIDDEN_CHUNKS, width_in),
        in_specs=[SMEM, VMEM, VMEM],
        out_specs=[VMEM] * len(HIDDEN_CHUNKS),
        compiler_params=params(32),
    )(my_half, routes_t, hidden_rows.transpose(1, 0, 2))
    packed_g = pl.pallas_call(
        pack_grad_kernel,
        out_shape=packed_shapes(GRAD_CHUNKS, width_out),
        in_specs=[SMEM, VMEM, VMEM, VMEM],
        out_specs=[VMEM] * len(GRAD_CHUNKS),
        compiler_params=params(32),
    )(my_half, routes_t, gates.T, out_grads)
    panel = jnp.concatenate([panel_a[0], panel_g[0]], axis=1)
    panels = [panel] + [
        lax.ppermute(panel, ("yl", "core"), [(i, i ^ away) for i in range(OWNERS)]) for away in range(1, OWNERS)
    ]
    chunks = [(packed_h[n], last - first, width_in) for n, (first, last) in enumerate(HIDDEN_CHUNKS)]
    chunks += [(packed_g[n], last - first, width_out) for n, (first, last) in enumerate(GRAD_CHUNKS)]
    rows = []
    before = None
    for sent, width, features in chunks:
        if before is not None:
            before, sent = lax.optimization_barrier((before, sent))
            rows.append(along_y(*gathered(before, *held)))
        before = lax.all_to_all(sent, ("x", "z"), 0, 0, tiled=True)
        held = (width, features)
    rows.append(along_y(*gathered(before, *held)))
    rows_h = [piece for part in rows[: len(HIDDEN_CHUNKS)] for piece in part]
    rows_g = [piece for part in rows[len(HIDDEN_CHUNKS) :] for piece in part]
    input_cov, input_panel = stats(quarter, panels, 0, rows_h, norm, 512)
    grad_cov, grad_panel = stats(quarter, panels, width_in // OWNERS, rows_g, norm, 512)
    return (input_cov[None], grad_cov[None], input_panel[None], grad_panel[None])


def solution(mesh):
    split = Mesh(mesh.devices.reshape(4, 2, 2, 2, Z), AXES)
    return jax.shard_map(
        per_device,
        mesh=split,
        in_specs=(
            P(AXES, None, None),
            P(AXES, None),
            P(AXES, None),
            P(AXES, None),
            P(AXES, None, None),
            P(AXES, None, None),
        ),
        out_specs=(P(AXES, None, None),) * 4,
        check_vma=False,
    )
```

```python
import functools

import jax
import jax.numpy as jnp
from jax import lax
from jax.experimental import pallas as pl
from jax.experimental.pallas import tpu as pltpu
from jax.sharding import Mesh
from jax.sharding import PartitionSpec as P

ROUTED = 160
OWNERS = 4
Z = 8
DESTS = 32
FLIGHT = 64
AXES = ("x", "yh", "yl", "core", "z")
SPLITS = {2: (4, 1), 4: (2, 2), 6: (4, 2)}
GRAD_FIRST = (0, 4)
GRAD_LAST = (4, 6)
HIDDEN_FIRST = (0, 4)
HIDDEN_LAST = (4, 6)
f32 = jnp.float32
bf16 = jnp.bfloat16
VMEM = pl.BlockSpec(memory_space=pltpu.VMEM)
SMEM = pl.BlockSpec(memory_space=pltpu.SMEM)
HBM = pl.BlockSpec(memory_space=pltpu.HBM)


def params(mib):
    return pltpu.CompilerParams(vmem_limit_bytes=mib * 2**20)


def one_hot(rows, target):
    position = lax.broadcasted_iota(jnp.int32, (rows, target.shape[1]), 0)
    return (position == target).astype(f32).astype(bf16)


def slot_table(routes_ref):
    slots, tok = routes_ref.shape
    ids = routes_ref[...]
    upper = (
        lax.broadcasted_iota(jnp.int32, (tok, tok), 0) < lax.broadcasted_iota(jnp.int32, (tok, tok), 1)
    ).astype(f32).astype(bf16)
    window = lax.broadcasted_iota(jnp.int32, (FLIGHT, tok), 0)
    seen = jnp.zeros((FLIGHT, 1), f32)
    out = []
    for k in range(slots):
        named = (window == ids[k : k + 1, :]).astype(f32)
        before = jnp.dot(named.astype(bf16), upper, preferred_element_type=f32) + seen
        slot = jnp.sum(named * before, axis=0, keepdims=True)
        seen = seen + jnp.sum(named, axis=1, keepdims=True)
        out.append((ids[k : k + 1, :], slot.astype(jnp.int32)))
    return out


def targets(table, my_half, first, last):
    width = last - first
    out = []
    for ids, slot in table:
        dest = lax.shift_right_logical(ids, 4) * Z + (ids & (Z - 1))
        across = (lax.shift_right_logical(ids, 3) & 1) ^ my_half
        place = across * (DESTS * width) + dest * width + slot - first
        ok = (ids < FLIGHT) & (slot >= first) & (slot < last)
        out.append(jnp.where(ok, place, -1))
    return out


def spread(own, across, width, out_ref):
    cuts, groups = SPLITS[width]
    block = cuts * 2 * width
    per = DESTS // groups
    lanes = out_ref.shape[2]
    source = lax.broadcasted_iota(jnp.int32, (1, 2 * per * width), 1)
    half = lax.div(source, per * width)
    rest = source - half * (per * width)
    dest = lax.div(rest, width)
    start = dest * block + half * width + rest - dest * width
    moves = [one_hot(per * block, start + cut * 2 * width) for cut in range(cuts)]
    for group in range(groups):
        here = slice(group * per * width, (group + 1) * per * width)
        both = jnp.concatenate([own[here, :], across[here, :]], axis=0)
        total = None
        for cut, move in enumerate(moves):
            part = jnp.dot(move, both[:, cut * lanes : (cut + 1) * lanes], preferred_element_type=f32)
            total = part if total is None else total + part
        out_ref[group * per : (group + 1) * per] = total.astype(bf16).reshape(per, block, lanes)


def packed_grads(table, half_ref, gates_ref, grads_ref, first, last):
    rows = FLIGHT * (last - first)
    position = lax.broadcasted_iota(jnp.int32, (rows, grads_ref.shape[0]), 0)
    pick = jnp.zeros(position.shape, f32)
    weight = jnp.zeros(position.shape, f32)
    for k, target in enumerate(targets(table, half_ref[0, 0], first, last)):
        hit = position == target
        pick = jnp.where(hit, 1.0, pick)
        weight = jnp.where(hit, gates_ref[k : k + 1, :], weight)
    gate = jnp.sum(weight, axis=1, keepdims=True)
    picked = jnp.dot(pick.astype(bf16), grads_ref[...], preferred_element_type=f32)
    return (gate * picked).astype(bf16)


def first_grads_kernel(half_ref, routes_ref, gates_ref, grads_ref, out_ref):
    packed = packed_grads(slot_table(routes_ref), half_ref, gates_ref, grads_ref, *GRAD_FIRST)
    rows = packed.shape[0] // 2
    spread(packed[:rows], packed[rows:], GRAD_FIRST[1] - GRAD_FIRST[0], out_ref)


def last_grads_kernel(half_ref, routes_ref, gates_ref, grads_ref, own_ref, across_ref):
    packed = packed_grads(slot_table(routes_ref), half_ref, gates_ref, grads_ref, *GRAD_LAST)
    rows = own_ref.shape[0]
    own_ref[...] = packed[:rows]
    across_ref[...] = packed[rows:]


def hidden_kernel(half_ref, routes_ref, hidden_ref, *outs):
    table = slot_table(routes_ref)
    for number, (first, last) in enumerate((HIDDEN_FIRST, HIDDEN_LAST)):
        rows = DESTS * (last - first)
        picked = None
        for k, target in enumerate(targets(table, half_ref[0, 0], first, last)):
            part = jnp.dot(one_hot(2 * rows, target), hidden_ref[k], preferred_element_type=f32)
            picked = part if picked is None else picked + part
        outs[2 * number][...] = picked[:rows].astype(bf16)
        outs[2 * number + 1][...] = picked[rows:].astype(bf16)


def block_shape(width, features):
    cuts = SPLITS[width][0]
    return jax.ShapeDtypeStruct((DESTS, cuts * 2 * width, features // cuts), bf16)


def rows_shape(width, features):
    return jax.ShapeDtypeStruct((DESTS * width, features), bf16)


def spread_kernel(width, own_ref, across_ref, out_ref):
    spread(own_ref, across_ref, width, out_ref)


def spread_rows(own, across, width):
    rows, features = own.shape
    return pl.pallas_call(
        functools.partial(spread_kernel, width),
        out_shape=block_shape(width, features),
        in_specs=[VMEM, VMEM],
        out_specs=VMEM,
        compiler_params=params(32),
        cost_estimate=pl.CostEstimate(flops=1, bytes_accessed=1, transcendentals=0),
    )(own, across)


def gather_kernel(width, in_ref, *outs):
    cuts, groups = SPLITS[width]
    block = cuts * 2 * width
    per = DESTS // groups
    lanes = in_ref.shape[2]
    source = lax.broadcasted_iota(jnp.int32, (1, per * block), 1)
    sender = lax.div(source, block)
    rest = source - sender * block
    cut_of = lax.div(rest, 2 * width)
    rest = rest - cut_of * (2 * width)
    half = lax.div(rest, width)
    place = half * (per * width) + sender * width + rest - half * width
    moves = [one_hot(2 * per * width, jnp.where(cut_of == cut, place, -1)) for cut in range(cuts)]
    for group in range(groups):
        piece = in_ref[group * per : (group + 1) * per].reshape(per * block, lanes)
        for cut, move in enumerate(moves):
            moved = jnp.dot(move, piece, preferred_element_type=f32).astype(bf16)
            there = slice(cut * lanes, (cut + 1) * lanes)
            if len(outs) == 2:
                here = slice(group * per * width, (group + 1) * per * width)
                outs[0][here, there] = moved[: per * width]
                outs[1][here, there] = moved[per * width :]
            else:
                outs[0][group * 2 * per * width : (group + 1) * 2 * per * width, there] = moved


def gathered(arrived, width, features, parts):
    rows = DESTS * width
    return pl.pallas_call(
        functools.partial(gather_kernel, width),
        out_shape=(jax.ShapeDtypeStruct((2 * rows // parts, features), bf16),) * parts,
        in_specs=[VMEM],
        out_specs=(VMEM,) * parts,
        compiler_params=params(32),
        cost_estimate=pl.CostEstimate(flops=1, bytes_accessed=1, transcendentals=0),
    )(arrived)


def thirds(value):
    high = value.astype(bf16)
    rest = value - high.astype(f32)
    middle = rest.astype(bf16)
    low = (rest - middle.astype(f32)).astype(bf16)
    return jnp.concatenate([high, middle, low], axis=0)


def added(value, rows):
    return value[:rows] + value[rows : 2 * rows] + value[2 * rows :]


def stats_kernel(norm, offset, count, more, q_ref, *refs):
    panels, rows = refs[:OWNERS], refs[OWNERS : OWNERS + count]
    before = refs[OWNERS + count : OWNERS + count + 2] if more else None
    cov_ref, out_ref, held, turned, sems = refs[-5:]
    block, tile = cov_ref.shape
    panel_rows = out_ref.shape[0]
    step = pl.program_id(0)
    quarter = q_ref[0, 0]

    def columns(away):
        return pl.ds(pl.multiple_of((quarter ^ away) * block, 128), block)

    @pl.when(step == 0)
    def _():
        copies = []
        at = 0
        for number, row in enumerate(rows):
            size = row.shape[0]
            copy = pltpu.make_async_copy(row, held.at[at : at + size, :], sems.at[number])
            copy.start()
            copies.append((copy, at, size))
            at += size
        for copy, at, size in copies:
            copy.wait()
        turned[...] = held[:, columns(0)].T

    tile_at = pl.ds(pl.multiple_of(step * tile, 128), tile)
    cov = jnp.dot(turned[...], held[:, tile_at], preferred_element_type=f32) * norm
    cov_ref[...] = cov + before[0][...] if more else cov

    @pl.when(step == pl.num_programs(0) - 1)
    def _():
        share = None
        for away in range(OWNERS):
            part = lax.dot_general(
                thirds(panels[away][:, offset : offset + block]),
                held[:, columns(away)],
                (((1,), (1,)), ((), ())),
                preferred_element_type=f32,
            )
            share = part if share is None else share + part
        product = jnp.dot(thirds(added(share, panel_rows)), held[:, columns(0)], preferred_element_type=f32)
        result = added(product, panel_rows) * norm
        out_ref[...] = result + before[1][...] if more else result


def stats(quarter, panels, offset, rows, norm, tile, before=None):
    features = rows[0].shape[1]
    block = features // OWNERS
    total = sum(row.shape[0] for row in rows)
    panel_rows, panel_width = panels[0].shape
    cov_spec = pl.BlockSpec((block, tile), lambda n: (0, n))
    out_spec = pl.BlockSpec((panel_rows, block), lambda n: (0, 0))
    more = before is not None
    return pl.pallas_call(
        functools.partial(stats_kernel, norm, offset, len(rows), more),
        grid=(features // tile,),
        out_shape=(
            jax.ShapeDtypeStruct((block, features), f32),
            jax.ShapeDtypeStruct((panel_rows, block), f32),
        ),
        in_specs=[SMEM]
        + [pl.BlockSpec((panel_rows, panel_width), lambda n: (0, 0))] * OWNERS
        + [HBM] * len(rows)
        + ([cov_spec, out_spec] if more else []),
        out_specs=(cov_spec, out_spec),
        scratch_shapes=[
            pltpu.VMEM((total, features), bf16),
            pltpu.VMEM((block, total), bf16),
            pltpu.SemaphoreType.DMA((len(rows),)),
        ],
        compiler_params=params(40),
        cost_estimate=pl.CostEstimate(flops=1, bytes_accessed=1, transcendentals=0),
    )(quarter, *panels, *rows, *(before or ()))


def core_swapped(value):
    return lax.ppermute(value, "core", [(0, 1), (1, 0)])


def y_moved(value, flip):
    return lax.ppermute(value, ("yh", "yl"), [(i, i ^ flip) for i in range(4)])


def along_xz(value):
    return lax.all_to_all(value, ("x", "z"), 0, 0, tiled=True)


def per_device(hidden_rows, out_grads, gates, routes, panel_a, panel_g):
    tok, slots, width_in = hidden_rows.shape
    width_out = out_grads.shape[1]
    norm = ROUTED / (tok * 256 * slots)
    routes_t = routes.T
    gates_t = gates.T
    my_half = lax.axis_index("yh").astype(jnp.int32).reshape(1, 1)
    quarter = (lax.axis_index("yl") * 2 + lax.axis_index("core")).astype(jnp.int32).reshape(1, 1)
    first, last = GRAD_FIRST[1] - GRAD_FIRST[0], GRAD_LAST[1] - GRAD_LAST[0]
    begin, rest = HIDDEN_FIRST[1] - HIDDEN_FIRST[0], HIDDEN_LAST[1] - HIDDEN_LAST[0]
    sent_a = pl.pallas_call(
        first_grads_kernel,
        out_shape=block_shape(first, width_out),
        in_specs=[SMEM, VMEM, VMEM, VMEM],
        out_specs=VMEM,
        compiler_params=params(32),
    )(my_half, routes_t, gates_t, out_grads)
    own_b, across_b = pl.pallas_call(
        last_grads_kernel,
        out_shape=(rows_shape(last, width_out),) * 2,
        in_specs=[SMEM, VMEM, VMEM, VMEM],
        out_specs=(VMEM, VMEM),
        compiler_params=params(32),
    )(my_half, routes_t, gates_t, out_grads)
    own_c, across_c, own_d, across_d = pl.pallas_call(
        hidden_kernel,
        out_shape=(rows_shape(begin, width_in),) * 2 + (rows_shape(rest, width_in),) * 2,
        in_specs=[SMEM, VMEM, VMEM],
        out_specs=(VMEM,) * 4,
        compiler_params=params(32),
    )(my_half, routes_t, hidden_rows.transpose(1, 0, 2))
    panel = jnp.concatenate([panel_a[0], panel_g[0]], axis=1)
    panels = [panel] + [
        lax.ppermute(panel, ("yl", "core"), [(i, i ^ away) for i in range(OWNERS)]) for away in range(1, OWNERS)
    ]
    sent_b = spread_rows(own_b, y_moved(across_b, 3), last)
    sent_c = spread_rows(own_c, y_moved(across_c, 3), begin)
    sent_d = spread_rows(own_d, y_moved(across_d, 3), rest)
    tie = lax.optimization_barrier

    got_a = along_xz(sent_a)
    got_a, sent_b, sent_c, sent_d, panels = tie((got_a, sent_b, sent_c, sent_d, panels))
    got_b = along_xz(sent_b)
    own_a, across_a = gathered(got_a, first, width_out, 2)
    beside_a, crossed_a = y_moved(own_a, 1), y_moved(across_a, 3)
    got_b, sent_c, beside_a, crossed_a = tie((got_b, sent_c, beside_a, crossed_a))
    got_c = along_xz(sent_c)
    relayed_a = y_moved(crossed_a, 1)
    (own_b,) = gathered(got_b, last, width_out, 1)
    beside_b = y_moved(own_b, 1)
    got_c, sent_d, relayed_a = tie((got_c, sent_d, relayed_a))
    got_d = along_xz(sent_d)
    rows_g = [own_a, beside_a, crossed_a, relayed_a, own_b, beside_b]
    rows_g = rows_g + [core_swapped(piece) for piece in rows_g]
    (own_c,) = gathered(got_c, begin, width_in, 1)
    beside_c = y_moved(own_c, 1)
    grad_cov, grad_panel = stats(quarter, panels, width_in // OWNERS, rows_g, norm, 1280)
    got_d, grad_cov, grad_panel = tie((got_d, grad_cov, grad_panel))
    (own_d,) = gathered(got_d, rest, width_in, 1)
    beside_d = y_moved(own_d, 1)
    rows_c = [own_c, beside_c, core_swapped(own_c), core_swapped(beside_c)]
    own_d, rows_c = tie((own_d, rows_c))
    partial = stats(quarter, panels, 0, rows_c, norm, 768)
    beside_d, partial = tie((beside_d, partial))
    rows_d = [own_d, beside_d, core_swapped(own_d), core_swapped(beside_d)]
    input_cov, input_panel = stats(quarter, panels, 0, rows_d, norm, 768, partial)
    return (input_cov[None], grad_cov[None], input_panel[None], grad_panel[None])


def solution(mesh):
    split = Mesh(mesh.devices.reshape(4, 2, 2, 2, Z), AXES)
    return jax.shard_map(
        per_device,
        mesh=split,
        in_specs=(
            P(AXES, None, None),
            P(AXES, None),
            P(AXES, None),
            P(AXES, None),
            P(AXES, None, None),
            P(AXES, None, None),
        ),
        out_specs=(P(AXES, None, None),) * 4,
        check_vma=False,
    )
```

```python
import functools

import jax
import jax.numpy as jnp
from jax import lax
from jax.experimental import pallas as pl
from jax.experimental.pallas import tpu as pltpu
from jax.sharding import Mesh
from jax.sharding import PartitionSpec as P

ROUTED = 160
OWNERS = 4
Z = 8
DESTS = 32
FLIGHT = 64
AXES = ("x", "yh", "yl", "core", "z")
SPLITS = {2: (4, 1), 4: (2, 2), 6: (4, 2)}
GRAD_FIRST = (0, 4)
GRAD_LAST = (4, 6)
HIDDEN_FIRST = (0, 4)
HIDDEN_LAST = (4, 6)
f32 = jnp.float32
bf16 = jnp.bfloat16
VMEM = pl.BlockSpec(memory_space=pltpu.VMEM)
SMEM = pl.BlockSpec(memory_space=pltpu.SMEM)
HBM = pl.BlockSpec(memory_space=pltpu.HBM)


def params(mib):
    return pltpu.CompilerParams(vmem_limit_bytes=mib * 2**20)


def one_hot(rows, target):
    position = lax.broadcasted_iota(jnp.int32, (rows, target.shape[1]), 0)
    return (position == target).astype(f32).astype(bf16)


def slot_table(routes_ref):
    slots, tok = routes_ref.shape
    ids = routes_ref[...]
    upper = (
        lax.broadcasted_iota(jnp.int32, (tok, tok), 0) < lax.broadcasted_iota(jnp.int32, (tok, tok), 1)
    ).astype(f32).astype(bf16)
    window = lax.broadcasted_iota(jnp.int32, (FLIGHT, tok), 0)
    seen = jnp.zeros((FLIGHT, 1), f32)
    out = []
    for k in range(slots):
        named = (window == ids[k : k + 1, :]).astype(f32)
        before = jnp.dot(named.astype(bf16), upper, preferred_element_type=f32) + seen
        slot = jnp.sum(named * before, axis=0, keepdims=True)
        seen = seen + jnp.sum(named, axis=1, keepdims=True)
        out.append((ids[k : k + 1, :], slot.astype(jnp.int32)))
    return out


def targets(table, my_half, first, last):
    width = last - first
    out = []
    for ids, slot in table:
        dest = lax.shift_right_logical(ids, 4) * Z + (ids & (Z - 1))
        across = (lax.shift_right_logical(ids, 3) & 1) ^ my_half
        place = across * (DESTS * width) + dest * width + slot - first
        ok = (ids < FLIGHT) & (slot >= first) & (slot < last)
        out.append(jnp.where(ok, place, -1))
    return out


def spread(own, across, width, out_ref):
    cuts, groups = SPLITS[width]
    block = cuts * 2 * width
    per = DESTS // groups
    lanes = out_ref.shape[2]
    source = lax.broadcasted_iota(jnp.int32, (1, 2 * per * width), 1)
    half = lax.div(source, per * width)
    rest = source - half * (per * width)
    dest = lax.div(rest, width)
    start = dest * block + half * width + rest - dest * width
    moves = [one_hot(per * block, start + cut * 2 * width) for cut in range(cuts)]
    for group in range(groups):
        here = slice(group * per * width, (group + 1) * per * width)
        both = jnp.concatenate([own[here, :], across[here, :]], axis=0)
        total = None
        for cut, move in enumerate(moves):
            part = jnp.dot(move, both[:, cut * lanes : (cut + 1) * lanes], preferred_element_type=f32)
            total = part if total is None else total + part
        out_ref[group * per : (group + 1) * per] = total.astype(bf16).reshape(per, block, lanes)


def packed_grads(table, half_ref, gates_ref, grads_ref, first, last):
    rows = FLIGHT * (last - first)
    position = lax.broadcasted_iota(jnp.int32, (rows, grads_ref.shape[0]), 0)
    pick = jnp.zeros(position.shape, f32)
    weight = jnp.zeros(position.shape, f32)
    for k, target in enumerate(targets(table, half_ref[0, 0], first, last)):
        hit = position == target
        pick = jnp.where(hit, 1.0, pick)
        weight = jnp.where(hit, gates_ref[k : k + 1, :], weight)
    gate = jnp.sum(weight, axis=1, keepdims=True)
    picked = jnp.dot(pick.astype(bf16), grads_ref[...], preferred_element_type=f32)
    return (gate * picked).astype(bf16)


def first_grads_kernel(half_ref, routes_ref, gates_ref, grads_ref, out_ref):
    packed = packed_grads(slot_table(routes_ref), half_ref, gates_ref, grads_ref, *GRAD_FIRST)
    rows = packed.shape[0] // 2
    spread(packed[:rows], packed[rows:], GRAD_FIRST[1] - GRAD_FIRST[0], out_ref)


def last_grads_kernel(half_ref, routes_ref, gates_ref, grads_ref, own_ref, across_ref):
    packed = packed_grads(slot_table(routes_ref), half_ref, gates_ref, grads_ref, *GRAD_LAST)
    rows = own_ref.shape[0]
    own_ref[...] = packed[:rows]
    across_ref[...] = packed[rows:]


def hidden_kernel(half_ref, routes_ref, hidden_ref, *outs):
    table = slot_table(routes_ref)
    for number, (first, last) in enumerate((HIDDEN_FIRST, HIDDEN_LAST)):
        rows = DESTS * (last - first)
        picked = None
        for k, target in enumerate(targets(table, half_ref[0, 0], first, last)):
            part = jnp.dot(one_hot(2 * rows, target), hidden_ref[k], preferred_element_type=f32)
            picked = part if picked is None else picked + part
        outs[2 * number][...] = picked[:rows].astype(bf16)
        outs[2 * number + 1][...] = picked[rows:].astype(bf16)


def block_shape(width, features):
    cuts = SPLITS[width][0]
    return jax.ShapeDtypeStruct((DESTS, cuts * 2 * width, features // cuts), bf16)


def rows_shape(width, features):
    return jax.ShapeDtypeStruct((DESTS * width, features), bf16)


def spread_kernel(width, own_ref, across_ref, out_ref):
    spread(own_ref, across_ref, width, out_ref)


def spread_rows(own, across, width):
    rows, features = own.shape
    return pl.pallas_call(
        functools.partial(spread_kernel, width),
        out_shape=block_shape(width, features),
        in_specs=[VMEM, VMEM],
        out_specs=VMEM,
        compiler_params=params(32),
        cost_estimate=pl.CostEstimate(flops=1, bytes_accessed=1, transcendentals=0),
    )(own, across)


def gather_kernel(width, in_ref, *outs):
    cuts, groups = SPLITS[width]
    block = cuts * 2 * width
    per = DESTS // groups
    lanes = in_ref.shape[2]
    source = lax.broadcasted_iota(jnp.int32, (1, per * block), 1)
    sender = lax.div(source, block)
    rest = source - sender * block
    cut_of = lax.div(rest, 2 * width)
    rest = rest - cut_of * (2 * width)
    half = lax.div(rest, width)
    place = half * (per * width) + sender * width + rest - half * width
    moves = [one_hot(2 * per * width, jnp.where(cut_of == cut, place, -1)) for cut in range(cuts)]
    for group in range(groups):
        piece = in_ref[group * per : (group + 1) * per].reshape(per * block, lanes)
        for cut, move in enumerate(moves):
            moved = jnp.dot(move, piece, preferred_element_type=f32).astype(bf16)
            there = slice(cut * lanes, (cut + 1) * lanes)
            if len(outs) == 2:
                here = slice(group * per * width, (group + 1) * per * width)
                outs[0][here, there] = moved[: per * width]
                outs[1][here, there] = moved[per * width :]
            else:
                outs[0][group * 2 * per * width : (group + 1) * 2 * per * width, there] = moved


def gathered(arrived, width, features, parts):
    rows = DESTS * width
    return pl.pallas_call(
        functools.partial(gather_kernel, width),
        out_shape=(jax.ShapeDtypeStruct((2 * rows // parts, features), bf16),) * parts,
        in_specs=[VMEM],
        out_specs=(VMEM,) * parts,
        compiler_params=params(32),
        cost_estimate=pl.CostEstimate(flops=1, bytes_accessed=1, transcendentals=0),
    )(arrived)


def thirds(value):
    high = value.astype(bf16)
    rest = value - high.astype(f32)
    middle = rest.astype(bf16)
    low = (rest - middle.astype(f32)).astype(bf16)
    return jnp.concatenate([high, middle, low], axis=0)


def added(value, rows):
    return value[:rows] + value[rows : 2 * rows] + value[2 * rows :]


def stats_kernel(norm, offset, count, more, q_ref, *refs):
    panels, rows = refs[:OWNERS], refs[OWNERS : OWNERS + count]
    before = refs[OWNERS + count : OWNERS + count + 2] if more else None
    cov_ref, out_ref, held, turned, sems = refs[-5:]
    block, tile = cov_ref.shape
    panel_rows = out_ref.shape[0]
    step = pl.program_id(0)
    quarter = q_ref[0, 0]

    def columns(away):
        return pl.ds(pl.multiple_of((quarter ^ away) * block, 128), block)

    @pl.when(step == 0)
    def _():
        copies = []
        at = 0
        for number, row in enumerate(rows):
            size = row.shape[0]
            copy = pltpu.make_async_copy(row, held.at[at : at + size, :], sems.at[number])
            copy.start()
            copies.append((copy, at, size))
            at += size
        for copy, at, size in copies:
            copy.wait()
        turned[...] = held[:, columns(0)].T

    tile_at = pl.ds(pl.multiple_of(step * tile, 128), tile)
    cov = jnp.dot(turned[...], held[:, tile_at], preferred_element_type=f32) * norm
    cov_ref[...] = cov + before[0][...] if more else cov

    @pl.when(step == pl.num_programs(0) - 1)
    def _():
        share = None
        for away in range(OWNERS):
            part = lax.dot_general(
                thirds(panels[away][:, offset : offset + block]),
                held[:, columns(away)],
                (((1,), (1,)), ((), ())),
                preferred_element_type=f32,
            )
            share = part if share is None else share + part
        product = jnp.dot(thirds(added(share, panel_rows)), held[:, columns(0)], preferred_element_type=f32)
        result = added(product, panel_rows) * norm
        out_ref[...] = result + before[1][...] if more else result


def stats(quarter, panels, offset, rows, norm, tile, before=None):
    features = rows[0].shape[1]
    block = features // OWNERS
    total = sum(row.shape[0] for row in rows)
    panel_rows, panel_width = panels[0].shape
    cov_spec = pl.BlockSpec((block, tile), lambda n: (0, n))
    out_spec = pl.BlockSpec((panel_rows, block), lambda n: (0, 0))
    more = before is not None
    return pl.pallas_call(
        functools.partial(stats_kernel, norm, offset, len(rows), more),
        grid=(features // tile,),
        out_shape=(
            pltpu.HBM((block, features), f32),
            jax.ShapeDtypeStruct((panel_rows, block), f32),
        ),
        in_specs=[SMEM]
        + [pl.BlockSpec((panel_rows, panel_width), lambda n: (0, 0))] * OWNERS
        + [HBM] * len(rows)
        + ([cov_spec, out_spec] if more else []),
        out_specs=(cov_spec, out_spec),
        scratch_shapes=[
            pltpu.VMEM((total, features), bf16),
            pltpu.VMEM((block, total), bf16),
            pltpu.SemaphoreType.DMA((len(rows),)),
        ],
        input_output_aliases={1 + OWNERS + len(rows): 0, 2 + OWNERS + len(rows): 1} if more else {},
        compiler_params=params(40),
        cost_estimate=pl.CostEstimate(flops=1, bytes_accessed=1, transcendentals=0),
    )(quarter, *panels, *rows, *(before or ()))


def core_swapped(value):
    return lax.ppermute(value, "core", [(0, 1), (1, 0)])


def y_moved(value, flip):
    return lax.ppermute(value, ("yh", "yl"), [(i, i ^ flip) for i in range(4)])


def after(value, *events):
    return lax.optimization_barrier((value, events))[0]


def along_xz(value):
    return lax.all_to_all(value, ("x", "z"), 0, 0, tiled=True)


def per_device(hidden_rows, out_grads, gates, routes, panel_a, panel_g):
    tok, slots, width_in = hidden_rows.shape
    width_out = out_grads.shape[1]
    norm = ROUTED / (tok * 256 * slots)
    routes_t = routes.T
    gates_t = gates.T
    my_half = lax.axis_index("yh").astype(jnp.int32).reshape(1, 1)
    quarter = (lax.axis_index("yl") * 2 + lax.axis_index("core")).astype(jnp.int32).reshape(1, 1)
    first, last = GRAD_FIRST[1] - GRAD_FIRST[0], GRAD_LAST[1] - GRAD_LAST[0]
    begin, rest = HIDDEN_FIRST[1] - HIDDEN_FIRST[0], HIDDEN_LAST[1] - HIDDEN_LAST[0]
    sent_a = pl.pallas_call(
        first_grads_kernel,
        out_shape=block_shape(first, width_out),
        in_specs=[SMEM, VMEM, VMEM, VMEM],
        out_specs=VMEM,
        compiler_params=params(32),
    )(my_half, routes_t, gates_t, out_grads)
    own_b, across_b = pl.pallas_call(
        last_grads_kernel,
        out_shape=(rows_shape(last, width_out),) * 2,
        in_specs=[SMEM, VMEM, VMEM, VMEM],
        out_specs=(VMEM, VMEM),
        compiler_params=params(32),
    )(my_half, routes_t, gates_t, out_grads)
    own_c, across_c, own_d, across_d = pl.pallas_call(
        hidden_kernel,
        out_shape=(rows_shape(begin, width_in),) * 2 + (rows_shape(rest, width_in),) * 2,
        in_specs=[SMEM, VMEM, VMEM],
        out_specs=(VMEM,) * 4,
        compiler_params=params(32),
    )(my_half, routes_t, hidden_rows.transpose(1, 0, 2))
    panel = jnp.concatenate([panel_a[0], panel_g[0]], axis=1)
    panels = [panel] + [
        lax.ppermute(panel, ("yl", "core"), [(i, i ^ away) for i in range(OWNERS)]) for away in range(1, OWNERS)
    ]
    sent_b = spread_rows(own_b, y_moved(across_b, 3), last)
    sent_c = spread_rows(own_c, y_moved(across_c, 3), begin)
    sent_d = spread_rows(own_d, y_moved(across_d, 3), rest)

    got_a = along_xz(sent_a)
    got_a, sent_b, sent_c, sent_d, panels = lax.optimization_barrier((got_a, sent_b, sent_c, sent_d, panels))
    got_b = along_xz(sent_b)
    own_a, across_a = gathered(got_a, first, width_out, 2)
    beside_a, crossed_a = y_moved(own_a, 1), y_moved(across_a, 3)
    got_c = along_xz(after(sent_c, got_b, beside_a, crossed_a))
    relayed_a = y_moved(crossed_a, 1)
    (own_b,) = gathered(got_b, last, width_out, 1)
    beside_b = y_moved(own_b, 1)
    rows_a = [own_a, beside_a, crossed_a]
    rows_a = rows_a + [core_swapped(piece) for piece in rows_a]
    begun_g = stats(quarter, panels, width_in // OWNERS, after(rows_a, own_b), norm, 1280)
    got_c, sent_d, relayed_a = lax.optimization_barrier((got_c, sent_d, relayed_a))
    swapped_a = core_swapped(relayed_a)
    got_d = along_xz(sent_d)
    (own_c,) = gathered(after(got_c, begun_g), begin, width_in, 1)
    beside_c = y_moved(own_c, 1)
    rows_b = [relayed_a, swapped_a, own_b, beside_b, core_swapped(own_b), core_swapped(beside_b)]
    grad_cov, grad_panel = stats(quarter, panels, width_in // OWNERS, rows_b, norm, 1280, begun_g)
    (own_d,) = gathered(after(got_d, grad_cov), rest, width_in, 1)
    beside_d = y_moved(own_d, 1)
    own_c, beside_c = after((own_c, beside_c), own_d)
    rows_c = [own_c, beside_c, core_swapped(own_c), core_swapped(beside_c)]
    begun_h = stats(quarter, panels, 0, rows_c, norm, 768)
    beside_d = after(beside_d, begun_h)
    rows_d = [own_d, beside_d, core_swapped(own_d), core_swapped(beside_d)]
    input_cov, input_panel = stats(quarter, panels, 0, rows_d, norm, 768, begun_h)
    return (input_cov[None], grad_cov[None], input_panel[None], grad_panel[None])


def solution(mesh):
    split = Mesh(mesh.devices.reshape(4, 2, 2, 2, Z), AXES)
    return jax.shard_map(
        per_device,
        mesh=split,
        in_specs=(
            P(AXES, None, None),
            P(AXES, None),
            P(AXES, None),
            P(AXES, None),
            P(AXES, None, None),
            P(AXES, None, None),
        ),
        out_specs=(P(AXES, None, None),) * 4,
        check_vma=False,
    )
```

```python
import functools

import jax
import jax.numpy as jnp
from jax import lax
from jax.experimental import pallas as pl
from jax.experimental.pallas import tpu as pltpu
from jax.sharding import Mesh
from jax.sharding import PartitionSpec as P

ROUTED = 160
OWNERS = 4
Z = 8
DESTS = 32
FLIGHT = 64
AXES = ("x", "yh", "yl", "core", "z")
SPLITS = {2: (4, 1), 4: (2, 2), 6: (4, 2)}
GRAD_FIRST = (0, 4)
GRAD_LAST = (4, 6)
HIDDEN = (0, 6)
f32 = jnp.float32
bf16 = jnp.bfloat16
VMEM = pl.BlockSpec(memory_space=pltpu.VMEM)
SMEM = pl.BlockSpec(memory_space=pltpu.SMEM)
HBM = pl.BlockSpec(memory_space=pltpu.HBM)


def params(mib):
    return pltpu.CompilerParams(vmem_limit_bytes=mib * 2**20)


def one_hot(rows, target):
    position = lax.broadcasted_iota(jnp.int32, (rows, target.shape[1]), 0)
    return (position == target).astype(f32).astype(bf16)


def slot_table(routes_ref):
    slots, tok = routes_ref.shape
    ids = routes_ref[...]
    upper = (
        lax.broadcasted_iota(jnp.int32, (tok, tok), 0) < lax.broadcasted_iota(jnp.int32, (tok, tok), 1)
    ).astype(f32).astype(bf16)
    window = lax.broadcasted_iota(jnp.int32, (FLIGHT, tok), 0)
    seen = jnp.zeros((FLIGHT, 1), f32)
    out = []
    for k in range(slots):
        named = (window == ids[k : k + 1, :]).astype(f32)
        before = jnp.dot(named.astype(bf16), upper, preferred_element_type=f32) + seen
        slot = jnp.sum(named * before, axis=0, keepdims=True)
        seen = seen + jnp.sum(named, axis=1, keepdims=True)
        out.append((ids[k : k + 1, :], slot.astype(jnp.int32)))
    return out


def targets(table, my_half, first, last):
    width = last - first
    out = []
    for ids, slot in table:
        dest = lax.shift_right_logical(ids, 4) * Z + (ids & (Z - 1))
        across = (lax.shift_right_logical(ids, 3) & 1) ^ my_half
        place = across * (DESTS * width) + dest * width + slot - first
        ok = (ids < FLIGHT) & (slot >= first) & (slot < last)
        out.append(jnp.where(ok, place, -1))
    return out


def spread(own, across, width, out_ref):
    cuts, groups = SPLITS[width]
    block = cuts * 2 * width
    per = DESTS // groups
    lanes = out_ref.shape[2]
    source = lax.broadcasted_iota(jnp.int32, (1, 2 * per * width), 1)
    half = lax.div(source, per * width)
    rest = source - half * (per * width)
    dest = lax.div(rest, width)
    start = dest * block + half * width + rest - dest * width
    moves = [one_hot(per * block, start + cut * 2 * width) for cut in range(cuts)]
    for group in range(groups):
        here = slice(group * per * width, (group + 1) * per * width)
        both = jnp.concatenate([own[here, :], across[here, :]], axis=0)
        total = None
        for cut, move in enumerate(moves):
            part = jnp.dot(move, both[:, cut * lanes : (cut + 1) * lanes], preferred_element_type=f32)
            total = part if total is None else total + part
        out_ref[group * per : (group + 1) * per] = total.astype(bf16).reshape(per, block, lanes)


def packed_grads(table, half_ref, gates_ref, grads_ref, first, last):
    rows = FLIGHT * (last - first)
    position = lax.broadcasted_iota(jnp.int32, (rows, grads_ref.shape[0]), 0)
    pick = jnp.zeros(position.shape, f32)
    weight = jnp.zeros(position.shape, f32)
    for k, target in enumerate(targets(table, half_ref[0, 0], first, last)):
        hit = position == target
        pick = jnp.where(hit, 1.0, pick)
        weight = jnp.where(hit, gates_ref[k : k + 1, :], weight)
    gate = jnp.sum(weight, axis=1, keepdims=True)
    picked = jnp.dot(pick.astype(bf16), grads_ref[...], preferred_element_type=f32)
    return (gate * picked).astype(bf16)


def hidden_kernel(half_ref, routes_ref, hidden_ref, out_ref):
    rows = FLIGHT * (HIDDEN[1] - HIDDEN[0])
    picked = None
    for k, target in enumerate(targets(slot_table(routes_ref), half_ref[0, 0], *HIDDEN)):
        part = jnp.dot(one_hot(rows, target), hidden_ref[k], preferred_element_type=f32)
        picked = part if picked is None else picked + part
    packed = picked.astype(bf16)
    spread(packed[: rows // 2], packed[rows // 2 :], HIDDEN[1] - HIDDEN[0], out_ref)


def grads_kernel(half_ref, routes_ref, gates_ref, grads_ref, *outs):
    table = slot_table(routes_ref)
    for number, (first, last) in enumerate((GRAD_FIRST, GRAD_LAST)):
        packed = packed_grads(table, half_ref, gates_ref, grads_ref, first, last)
        rows = packed.shape[0] // 2
        outs[2 * number][...] = packed[:rows]
        outs[2 * number + 1][...] = packed[rows:]


def block_shape(width, features):
    cuts = SPLITS[width][0]
    return jax.ShapeDtypeStruct((DESTS, cuts * 2 * width, features // cuts), bf16)


def rows_shape(width, features):
    return jax.ShapeDtypeStruct((DESTS * width, features), bf16)


def spread_kernel(width, own_ref, across_ref, out_ref):
    spread(own_ref, across_ref, width, out_ref)


def spread_rows(own, across, width):
    rows, features = own.shape
    return pl.pallas_call(
        functools.partial(spread_kernel, width),
        out_shape=block_shape(width, features),
        in_specs=[VMEM, VMEM],
        out_specs=VMEM,
        compiler_params=params(32),
        cost_estimate=pl.CostEstimate(flops=1, bytes_accessed=1, transcendentals=0),
    )(own, across)


def gather_kernel(width, in_ref, *outs):
    cuts, groups = SPLITS[width]
    block = cuts * 2 * width
    per = DESTS // groups
    lanes = in_ref.shape[2]
    source = lax.broadcasted_iota(jnp.int32, (1, per * block), 1)
    sender = lax.div(source, block)
    rest = source - sender * block
    cut_of = lax.div(rest, 2 * width)
    rest = rest - cut_of * (2 * width)
    half = lax.div(rest, width)
    place = half * (per * width) + sender * width + rest - half * width
    moves = [one_hot(2 * per * width, jnp.where(cut_of == cut, place, -1)) for cut in range(cuts)]
    for group in range(groups):
        piece = in_ref[group * per : (group + 1) * per].reshape(per * block, lanes)
        for cut, move in enumerate(moves):
            moved = jnp.dot(move, piece, preferred_element_type=f32).astype(bf16)
            there = slice(cut * lanes, (cut + 1) * lanes)
            if len(outs) == 2:
                here = slice(group * per * width, (group + 1) * per * width)
                outs[0][here, there] = moved[: per * width]
                outs[1][here, there] = moved[per * width :]
            else:
                outs[0][group * 2 * per * width : (group + 1) * 2 * per * width, there] = moved


def gathered(arrived, width, features, parts):
    rows = DESTS * width
    return pl.pallas_call(
        functools.partial(gather_kernel, width),
        out_shape=(jax.ShapeDtypeStruct((2 * rows // parts, features), bf16),) * parts,
        in_specs=[VMEM],
        out_specs=(VMEM,) * parts,
        compiler_params=params(32),
        cost_estimate=pl.CostEstimate(flops=1, bytes_accessed=1, transcendentals=0),
    )(arrived)


def thirds(value):
    high = value.astype(bf16)
    rest = value - high.astype(f32)
    middle = rest.astype(bf16)
    low = (rest - middle.astype(f32)).astype(bf16)
    return jnp.concatenate([high, middle, low], axis=0)


def added(value, rows):
    return value[:rows] + value[rows : 2 * rows] + value[2 * rows :]


def stats_kernel(norm, offset, count, more, q_ref, *refs):
    panels, rows = refs[:OWNERS], refs[OWNERS : OWNERS + count]
    before = refs[OWNERS + count : OWNERS + count + 2] if more else None
    cov_ref, out_ref, held, turned, sems = refs[-5:]
    block, tile = cov_ref.shape
    panel_rows = out_ref.shape[0]
    step = pl.program_id(0)
    quarter = q_ref[0, 0]

    def columns(away):
        return pl.ds(pl.multiple_of((quarter ^ away) * block, 128), block)

    @pl.when(step == 0)
    def _():
        copies = []
        at = 0
        for number, row in enumerate(rows):
            size = row.shape[0]
            copy = pltpu.make_async_copy(row, held.at[at : at + size, :], sems.at[number])
            copy.start()
            copies.append((copy, at, size))
            at += size
        for copy, at, size in copies:
            copy.wait()
        turned[...] = held[:, columns(0)].T

    tile_at = pl.ds(pl.multiple_of(step * tile, 128), tile)
    cov = jnp.dot(turned[...], held[:, tile_at], preferred_element_type=f32) * norm
    cov_ref[...] = cov + before[0][...] if more else cov

    @pl.when(step == pl.num_programs(0) - 1)
    def _():
        share = None
        for away in range(OWNERS):
            part = lax.dot_general(
                thirds(panels[away][:, offset : offset + block]),
                held[:, columns(away)],
                (((1,), (1,)), ((), ())),
                preferred_element_type=f32,
            )
            share = part if share is None else share + part
        product = jnp.dot(thirds(added(share, panel_rows)), held[:, columns(0)], preferred_element_type=f32)
        result = added(product, panel_rows) * norm
        out_ref[...] = result + before[1][...] if more else result


def stats(quarter, panels, offset, rows, norm, tile, before=None):
    features = rows[0].shape[1]
    block = features // OWNERS
    total = sum(row.shape[0] for row in rows)
    panel_rows, panel_width = panels[0].shape
    cov_spec = pl.BlockSpec((block, tile), lambda n: (0, n))
    out_spec = pl.BlockSpec((panel_rows, block), lambda n: (0, 0))
    more = before is not None
    return pl.pallas_call(
        functools.partial(stats_kernel, norm, offset, len(rows), more),
        grid=(features // tile,),
        out_shape=(
            pltpu.HBM((block, features), f32),
            jax.ShapeDtypeStruct((panel_rows, block), f32),
        ),
        in_specs=[SMEM]
        + [pl.BlockSpec((panel_rows, panel_width), lambda n: (0, 0))] * OWNERS
        + [HBM] * len(rows)
        + ([cov_spec, out_spec] if more else []),
        out_specs=(cov_spec, out_spec),
        scratch_shapes=[
            pltpu.VMEM((total, features), bf16),
            pltpu.VMEM((block, total), bf16),
            pltpu.SemaphoreType.DMA((len(rows),)),
        ],
        input_output_aliases={1 + OWNERS + len(rows): 0, 2 + OWNERS + len(rows): 1} if more else {},
        compiler_params=params(40),
        cost_estimate=pl.CostEstimate(flops=1, bytes_accessed=1, transcendentals=0),
    )(quarter, *panels, *rows, *(before or ()))


def core_swapped(value):
    return lax.ppermute(value, "core", [(0, 1), (1, 0)])


def y_moved(value, flip):
    return lax.ppermute(value, ("yh", "yl"), [(i, i ^ flip) for i in range(4)])


def after(value, *events):
    return lax.optimization_barrier((value, events))[0]


def along_xz(value):
    return lax.all_to_all(value, ("x", "z"), 0, 0, tiled=True)


def per_device(hidden_rows, out_grads, gates, routes, panel_a, panel_g):
    tok, slots, width_in = hidden_rows.shape
    width_out = out_grads.shape[1]
    norm = ROUTED / (tok * 256 * slots)
    routes_t = routes.T
    gates_t = gates.T
    my_half = lax.axis_index("yh").astype(jnp.int32).reshape(1, 1)
    quarter = (lax.axis_index("yl") * 2 + lax.axis_index("core")).astype(jnp.int32).reshape(1, 1)
    whole, first, last = (end - start for start, end in (HIDDEN, GRAD_FIRST, GRAD_LAST))
    sent_h = pl.pallas_call(
        hidden_kernel,
        out_shape=block_shape(whole, width_in),
        in_specs=[SMEM, VMEM, VMEM],
        out_specs=VMEM,
        compiler_params=params(32),
    )(my_half, routes_t, hidden_rows.transpose(1, 0, 2))
    own_b, across_b, own_c, across_c = pl.pallas_call(
        grads_kernel,
        out_shape=(rows_shape(first, width_out),) * 2 + (rows_shape(last, width_out),) * 2,
        in_specs=[SMEM, VMEM, VMEM, VMEM],
        out_specs=(VMEM,) * 4,
        compiler_params=params(32),
    )(my_half, routes_t, gates_t, out_grads)
    panel = jnp.concatenate([panel_a[0], panel_g[0]], axis=1)
    panels = [panel] + [
        lax.ppermute(panel, ("yl", "core"), [(i, i ^ away) for i in range(OWNERS)]) for away in range(1, OWNERS)
    ]
    sent_b = spread_rows(own_b, y_moved(across_b, 3), first)
    sent_c = spread_rows(own_c, y_moved(across_c, 3), last)
    at = width_in // OWNERS

    got_h = along_xz(sent_h)
    got_h, sent_b, sent_c, panels = lax.optimization_barrier((got_h, sent_b, sent_c, panels))
    got_b = along_xz(sent_b)
    own_h, across_h = gathered(got_h, whole, width_in, 2)
    beside_h, crossed_h = y_moved(own_h, 1), y_moved(across_h, 3)
    relayed_h = y_moved(crossed_h, 1)
    got_b = after(got_b, beside_h, relayed_h)
    sent_c = after(sent_c, got_b)
    rows_h = [own_h, beside_h, crossed_h, relayed_h]
    rows_h = rows_h + [core_swapped(piece) for piece in rows_h]
    (own_b,) = gathered(got_b, first, width_out, 1)
    beside_b = y_moved(own_b, 1)
    got_c = along_xz(sent_c)
    input_cov, input_panel = stats(quarter, panels, 0, after(rows_h, own_b), norm, 768)
    rows_b = after([own_b, core_swapped(own_b)], input_cov)
    begun_g = stats(quarter, panels, at, rows_b, norm, 1280)
    swapped_b = core_swapped(after(beside_b, begun_g))
    (own_c,) = gathered(after(got_c, begun_g), last, width_out, 1)
    beside_c = y_moved(own_c, 1)
    rows_d = after([beside_b, swapped_b, own_c, core_swapped(own_c)], own_c)
    going_g = stats(quarter, panels, at, rows_d, norm, 1280, begun_g)
    beside_c = after(beside_c, going_g)
    grad_cov, grad_panel = stats(quarter, panels, at, [beside_c, core_swapped(beside_c)], norm, 1280, going_g)
    return (input_cov[None], grad_cov[None], input_panel[None], grad_panel[None])


def solution(mesh):
    split = Mesh(mesh.devices.reshape(4, 2, 2, 2, Z), AXES)
    return jax.shard_map(
        per_device,
        mesh=split,
        in_specs=(
            P(AXES, None, None),
            P(AXES, None),
            P(AXES, None),
            P(AXES, None),
            P(AXES, None, None),
            P(AXES, None, None),
        ),
        out_specs=(P(AXES, None, None),) * 4,
        check_vma=False,
    )
```

```python
import functools

import jax
import jax.numpy as jnp
from jax import lax
from jax.experimental import pallas as pl
from jax.experimental.pallas import tpu as pltpu
from jax.sharding import Mesh
from jax.sharding import PartitionSpec as P

ROUTED = 160
OWNERS = 4
Z = 8
DESTS = 32
FLIGHT = 64
AXES = ("x", "yh", "yl", "core", "z")
SPLITS = {2: (4, 1), 4: (2, 2), 6: (4, 2)}
GRAD_FIRST = (0, 4)
GRAD_LAST = (4, 6)
HIDDEN = (0, 6)
f32 = jnp.float32
bf16 = jnp.bfloat16
VMEM = pl.BlockSpec(memory_space=pltpu.VMEM)
SMEM = pl.BlockSpec(memory_space=pltpu.SMEM)
HBM = pl.BlockSpec(memory_space=pltpu.HBM)


def params(mib):
    return pltpu.CompilerParams(vmem_limit_bytes=mib * 2**20)


def one_hot(rows, target):
    position = lax.broadcasted_iota(jnp.int32, (rows, target.shape[1]), 0)
    return (position == target).astype(f32).astype(bf16)


def slot_table(routes_ref):
    slots, tok = routes_ref.shape
    ids = routes_ref[...]
    upper = (
        lax.broadcasted_iota(jnp.int32, (tok, tok), 0) < lax.broadcasted_iota(jnp.int32, (tok, tok), 1)
    ).astype(f32).astype(bf16)
    window = lax.broadcasted_iota(jnp.int32, (FLIGHT, tok), 0)
    seen = jnp.zeros((FLIGHT, 1), f32)
    out = []
    for k in range(slots):
        named = (window == ids[k : k + 1, :]).astype(f32)
        before = jnp.dot(named.astype(bf16), upper, preferred_element_type=f32) + seen
        slot = jnp.sum(named * before, axis=0, keepdims=True)
        seen = seen + jnp.sum(named, axis=1, keepdims=True)
        out.append((ids[k : k + 1, :], slot.astype(jnp.int32)))
    return out


def targets(table, my_half, first, last):
    width = last - first
    out = []
    for ids, slot in table:
        dest = lax.shift_right_logical(ids, 4) * Z + (ids & (Z - 1))
        across = (lax.shift_right_logical(ids, 3) & 1) ^ my_half
        place = across * (DESTS * width) + dest * width + slot - first
        ok = (ids < FLIGHT) & (slot >= first) & (slot < last)
        out.append(jnp.where(ok, place, -1))
    return out


def spread(own, across, width, out_ref):
    cuts, groups = SPLITS[width]
    block = cuts * 2 * width
    per = DESTS // groups
    lanes = out_ref.shape[2]
    source = lax.broadcasted_iota(jnp.int32, (1, 2 * per * width), 1)
    half = lax.div(source, per * width)
    rest = source - half * (per * width)
    dest = lax.div(rest, width)
    start = dest * block + half * width + rest - dest * width
    move = jnp.concatenate([one_hot(per * block, start + cut * 2 * width) for cut in range(cuts)], axis=1)
    for group in range(groups):
        here = slice(group * per * width, (group + 1) * per * width)
        both = jnp.concatenate([own[here, :], across[here, :]], axis=0)
        stacked = jnp.concatenate([both[:, cut * lanes : (cut + 1) * lanes] for cut in range(cuts)], axis=0)
        total = jnp.dot(move, stacked, preferred_element_type=f32)
        out_ref[group * per : (group + 1) * per] = total.astype(bf16).reshape(per, block, lanes)


def packed_grads(table, half_ref, gates_ref, grads_ref, first, last):
    rows = FLIGHT * (last - first)
    position = lax.broadcasted_iota(jnp.int32, (rows, grads_ref.shape[0]), 0)
    pick = jnp.zeros(position.shape, f32)
    weight = jnp.zeros(position.shape, f32)
    for k, target in enumerate(targets(table, half_ref[0, 0], first, last)):
        hit = position == target
        pick = jnp.where(hit, 1.0, pick)
        weight = jnp.where(hit, gates_ref[k : k + 1, :], weight)
    gate = jnp.sum(weight, axis=1, keepdims=True)
    picked = jnp.dot(pick.astype(bf16), grads_ref[...], preferred_element_type=f32)
    return (gate * picked).astype(bf16)


def hidden_kernel(half_ref, routes_ref, hidden_ref, out_ref):
    rows = FLIGHT * (HIDDEN[1] - HIDDEN[0])
    places = targets(slot_table(routes_ref), half_ref[0, 0], *HIDDEN)
    picks = jnp.concatenate([one_hot(rows, target) for target in places], axis=1)
    entries = hidden_ref[...].reshape(picks.shape[1], hidden_ref.shape[2])
    packed = jnp.dot(picks, entries, preferred_element_type=f32).astype(bf16)
    spread(packed[: rows // 2], packed[rows // 2 :], HIDDEN[1] - HIDDEN[0], out_ref)


def grads_kernel(half_ref, routes_ref, gates_ref, grads_ref, *outs):
    table = slot_table(routes_ref)
    for number, (first, last) in enumerate((GRAD_FIRST, GRAD_LAST)):
        packed = packed_grads(table, half_ref, gates_ref, grads_ref, first, last)
        rows = packed.shape[0] // 2
        outs[2 * number][...] = packed[:rows]
        outs[2 * number + 1][...] = packed[rows:]


def block_shape(width, features):
    cuts = SPLITS[width][0]
    return jax.ShapeDtypeStruct((DESTS, cuts * 2 * width, features // cuts), bf16)


def rows_shape(width, features):
    return jax.ShapeDtypeStruct((DESTS * width, features), bf16)


def spread_kernel(width, own_ref, across_ref, out_ref):
    spread(own_ref, across_ref, width, out_ref)


def spread_rows(own, across, width):
    rows, features = own.shape
    return pl.pallas_call(
        functools.partial(spread_kernel, width),
        out_shape=block_shape(width, features),
        in_specs=[VMEM, VMEM],
        out_specs=VMEM,
        compiler_params=params(32),
        cost_estimate=pl.CostEstimate(flops=1, bytes_accessed=1, transcendentals=0),
    )(own, across)


def gather_kernel(width, in_ref, *outs):
    cuts, groups = SPLITS[width]
    block = cuts * 2 * width
    per = DESTS // groups
    lanes = in_ref.shape[2]
    source = lax.broadcasted_iota(jnp.int32, (1, per * block), 1)
    sender = lax.div(source, block)
    rest = source - sender * block
    cut_of = lax.div(rest, 2 * width)
    rest = rest - cut_of * (2 * width)
    half = lax.div(rest, width)
    place = half * (per * width) + sender * width + rest - half * width
    moves = [one_hot(2 * per * width, jnp.where(cut_of == cut, place, -1)) for cut in range(cuts)]
    for group in range(groups):
        piece = in_ref[group * per : (group + 1) * per].reshape(per * block, lanes)
        for cut, move in enumerate(moves):
            moved = jnp.dot(move, piece, preferred_element_type=f32).astype(bf16)
            there = slice(cut * lanes, (cut + 1) * lanes)
            if len(outs) == 2:
                here = slice(group * per * width, (group + 1) * per * width)
                outs[0][here, there] = moved[: per * width]
                outs[1][here, there] = moved[per * width :]
            else:
                outs[0][group * 2 * per * width : (group + 1) * 2 * per * width, there] = moved


def gathered(arrived, width, features, parts):
    rows = DESTS * width
    return pl.pallas_call(
        functools.partial(gather_kernel, width),
        out_shape=(jax.ShapeDtypeStruct((2 * rows // parts, features), bf16),) * parts,
        in_specs=[VMEM],
        out_specs=(VMEM,) * parts,
        compiler_params=params(32),
        cost_estimate=pl.CostEstimate(flops=1, bytes_accessed=1, transcendentals=0),
    )(arrived)


def thirds(value):
    high = value.astype(bf16)
    rest = value - high.astype(f32)
    middle = rest.astype(bf16)
    low = (rest - middle.astype(f32)).astype(bf16)
    return jnp.concatenate([high, middle, low], axis=0)


def added(value, rows):
    return value[:rows] + value[rows : 2 * rows] + value[2 * rows :]


def stats_kernel(norm, offset, count, more, q_ref, *refs):
    panels, rows = refs[:OWNERS], refs[OWNERS : OWNERS + count]
    before = refs[OWNERS + count : OWNERS + count + 2] if more else None
    cov_ref, out_ref, held, turned, sems = refs[-5:]
    block, tile = cov_ref.shape
    panel_rows = out_ref.shape[0]
    step = pl.program_id(0)
    quarter = q_ref[0, 0]

    def columns(away):
        return pl.ds(pl.multiple_of((quarter ^ away) * block, 128), block)

    @pl.when(step == 0)
    def _():
        copies = []
        at = 0
        for number, row in enumerate(rows):
            size = row.shape[0]
            copy = pltpu.make_async_copy(row, held.at[at : at + size, :], sems.at[number])
            copy.start()
            copies.append((copy, at, size))
            at += size
        for copy, at, size in copies:
            copy.wait()
        turned[...] = held[:, columns(0)].T

    tile_at = pl.ds(pl.multiple_of(step * tile, 128), tile)
    cov = jnp.dot(turned[...], held[:, tile_at], preferred_element_type=f32) * norm
    cov_ref[...] = cov + before[0][...] if more else cov

    @pl.when(step == pl.num_programs(0) - 1)
    def _():
        share = None
        for away in range(OWNERS):
            part = lax.dot_general(
                thirds(panels[away][:, offset : offset + block]),
                held[:, columns(away)],
                (((1,), (1,)), ((), ())),
                preferred_element_type=f32,
            )
            share = part if share is None else share + part
        product = jnp.dot(thirds(added(share, panel_rows)), held[:, columns(0)], preferred_element_type=f32)
        result = added(product, panel_rows) * norm
        out_ref[...] = result + before[1][...] if more else result


def stats(quarter, panels, offset, rows, norm, tile, before=None):
    features = rows[0].shape[1]
    block = features // OWNERS
    total = sum(row.shape[0] for row in rows)
    panel_rows, panel_width = panels[0].shape
    cov_spec = pl.BlockSpec((block, tile), lambda n: (0, n))
    out_spec = pl.BlockSpec((panel_rows, block), lambda n: (0, 0))
    more = before is not None
    return pl.pallas_call(
        functools.partial(stats_kernel, norm, offset, len(rows), more),
        grid=(features // tile,),
        out_shape=(
            pltpu.HBM((block, features), f32),
            jax.ShapeDtypeStruct((panel_rows, block), f32),
        ),
        in_specs=[SMEM]
        + [pl.BlockSpec((panel_rows, panel_width), lambda n: (0, 0))] * OWNERS
        + [HBM] * len(rows)
        + ([cov_spec, out_spec] if more else []),
        out_specs=(cov_spec, out_spec),
        scratch_shapes=[
            pltpu.VMEM((total, features), bf16),
            pltpu.VMEM((block, total), bf16),
            pltpu.SemaphoreType.DMA((len(rows),)),
        ],
        input_output_aliases={1 + OWNERS + len(rows): 0, 2 + OWNERS + len(rows): 1} if more else {},
        compiler_params=params(40),
        cost_estimate=pl.CostEstimate(flops=1, bytes_accessed=1, transcendentals=0),
    )(quarter, *panels, *rows, *(before or ()))


def core_swapped(value):
    return lax.ppermute(value, "core", [(0, 1), (1, 0)])


def y_moved(value, flip):
    return lax.ppermute(value, ("yh", "yl"), [(i, i ^ flip) for i in range(4)])


def after(value, *events):
    return lax.optimization_barrier((value, events))[0]


def along_xz(value):
    return lax.all_to_all(value, ("x", "z"), 0, 0, tiled=True)


def per_device(hidden_rows, out_grads, gates, routes, panel_a, panel_g):
    tok, slots, width_in = hidden_rows.shape
    width_out = out_grads.shape[1]
    norm = ROUTED / (tok * 256 * slots)
    routes_t = routes.T
    gates_t = gates.T
    my_half = lax.axis_index("yh").astype(jnp.int32).reshape(1, 1)
    quarter = (lax.axis_index("yl") * 2 + lax.axis_index("core")).astype(jnp.int32).reshape(1, 1)
    whole, first, last = (end - start for start, end in (HIDDEN, GRAD_FIRST, GRAD_LAST))
    sent_h = pl.pallas_call(
        hidden_kernel,
        out_shape=block_shape(whole, width_in),
        in_specs=[SMEM, VMEM, VMEM],
        out_specs=VMEM,
        compiler_params=params(32),
    )(my_half, routes_t, hidden_rows.transpose(1, 0, 2))
    own_b, across_b, own_c, across_c = pl.pallas_call(
        grads_kernel,
        out_shape=(rows_shape(first, width_out),) * 2 + (rows_shape(last, width_out),) * 2,
        in_specs=[SMEM, VMEM, VMEM, VMEM],
        out_specs=(VMEM,) * 4,
        compiler_params=params(32),
    )(my_half, routes_t, gates_t, out_grads)
    panel = jnp.concatenate([panel_a[0], panel_g[0]], axis=1)
    panels = [panel] + [
        lax.ppermute(panel, ("yl", "core"), [(i, i ^ away) for i in range(OWNERS)]) for away in range(1, OWNERS)
    ]
    sent_b = spread_rows(own_b, y_moved(across_b, 3), first)
    sent_c = spread_rows(own_c, y_moved(across_c, 3), last)
    at = width_in // OWNERS

    got_h = along_xz(sent_h)
    got_h, sent_b, sent_c, panels = lax.optimization_barrier((got_h, sent_b, sent_c, panels))
    got_b = along_xz(sent_b)
    own_h, across_h = gathered(got_h, whole, width_in, 2)
    beside_h, crossed_h = y_moved(own_h, 1), y_moved(across_h, 3)
    relayed_h = y_moved(crossed_h, 1)
    got_b = after(got_b, beside_h, relayed_h)
    sent_c = after(sent_c, got_b)
    rows_h = [own_h, beside_h, crossed_h, relayed_h]
    rows_h = rows_h + [core_swapped(piece) for piece in rows_h]
    (own_b,) = gathered(got_b, first, width_out, 1)
    beside_b = y_moved(own_b, 1)
    got_c = along_xz(sent_c)
    input_cov, input_panel = stats(quarter, panels, 0, after(rows_h, own_b), norm, 768)
    rows_b = after([own_b, core_swapped(own_b)], input_cov)
    begun_g = stats(quarter, panels, at, rows_b, norm, 1280)
    swapped_b = core_swapped(after(beside_b, begun_g))
    (own_c,) = gathered(after(got_c, begun_g), last, width_out, 1)
    beside_c = y_moved(own_c, 1)
    rows_d = after([beside_b, swapped_b, own_c, core_swapped(own_c)], own_c)
    going_g = stats(quarter, panels, at, rows_d, norm, 1280, begun_g)
    beside_c = after(beside_c, going_g)
    grad_cov, grad_panel = stats(quarter, panels, at, [beside_c, core_swapped(beside_c)], norm, 1280, going_g)
    return (input_cov[None], grad_cov[None], input_panel[None], grad_panel[None])


def solution(mesh):
    split = Mesh(mesh.devices.reshape(4, 2, 2, 2, Z), AXES)
    return jax.shard_map(
        per_device,
        mesh=split,
        in_specs=(
            P(AXES, None, None),
            P(AXES, None),
            P(AXES, None),
            P(AXES, None),
            P(AXES, None, None),
            P(AXES, None, None),
        ),
        out_specs=(P(AXES, None, None),) * 4,
        check_vma=False,
    )
```

```python
import functools

import jax
import jax.numpy as jnp
from jax import lax
from jax.experimental import pallas as pl
from jax.experimental.pallas import tpu as pltpu
from jax.sharding import Mesh
from jax.sharding import PartitionSpec as P

ROUTED = 160
OWNERS = 4
Z = 8
DESTS = 32
FLIGHT = 64
AXES = ("x", "yh", "yl", "core", "z")
SPLITS = {2: (4, 1), 4: (2, 2), 6: (4, 2)}
GRAD_FIRST = (0, 4)
GRAD_LAST = (4, 6)
HIDDEN = (0, 6)
f32 = jnp.float32
bf16 = jnp.bfloat16
VMEM = pl.BlockSpec(memory_space=pltpu.VMEM)
SMEM = pl.BlockSpec(memory_space=pltpu.SMEM)
HBM = pl.BlockSpec(memory_space=pltpu.HBM)


def params(mib):
    return pltpu.CompilerParams(vmem_limit_bytes=mib * 2**20)


def one_hot(rows, target):
    position = lax.broadcasted_iota(jnp.int32, (rows, target.shape[1]), 0)
    return (position == target).astype(f32).astype(bf16)


def slot_table(routes_ref):
    slots, tok = routes_ref.shape
    ids = routes_ref[...]
    upper = (
        lax.broadcasted_iota(jnp.int32, (tok, tok), 0) < lax.broadcasted_iota(jnp.int32, (tok, tok), 1)
    ).astype(f32).astype(bf16)
    window = lax.broadcasted_iota(jnp.int32, (FLIGHT, tok), 0)
    seen = jnp.zeros((FLIGHT, 1), f32)
    out = []
    for k in range(slots):
        named = (window == ids[k : k + 1, :]).astype(f32)
        before = jnp.dot(named.astype(bf16), upper, preferred_element_type=f32) + seen
        slot = jnp.sum(named * before, axis=0, keepdims=True)
        seen = seen + jnp.sum(named, axis=1, keepdims=True)
        out.append((ids[k : k + 1, :], slot.astype(jnp.int32)))
    return out


def targets(table, my_half, first, last):
    width = last - first
    out = []
    for ids, slot in table:
        dest = lax.shift_right_logical(ids, 4) * Z + (ids & (Z - 1))
        across = (lax.shift_right_logical(ids, 3) & 1) ^ my_half
        place = across * (DESTS * width) + dest * width + slot - first
        ok = (ids < FLIGHT) & (slot >= first) & (slot < last)
        out.append(jnp.where(ok, place, -1))
    return out


def spread(own, across, width, out_ref):
    cuts, groups = SPLITS[width]
    block = cuts * 2 * width
    per = DESTS // groups
    lanes = out_ref.shape[2]
    source = lax.broadcasted_iota(jnp.int32, (1, 2 * per * width), 1)
    half = lax.div(source, per * width)
    rest = source - half * (per * width)
    dest = lax.div(rest, width)
    start = dest * block + half * width + rest - dest * width
    move = jnp.concatenate([one_hot(per * block, start + cut * 2 * width) for cut in range(cuts)], axis=1)
    for group in range(groups):
        here = slice(group * per * width, (group + 1) * per * width)
        both = jnp.concatenate([own[here, :], across[here, :]], axis=0)
        stacked = jnp.concatenate([both[:, cut * lanes : (cut + 1) * lanes] for cut in range(cuts)], axis=0)
        total = jnp.dot(move, stacked, preferred_element_type=f32)
        out_ref[group * per : (group + 1) * per] = total.astype(bf16).reshape(per, block, lanes)


def packed_grads(table, half_ref, gates_ref, grads_ref, first, last):
    rows = FLIGHT * (last - first)
    position = lax.broadcasted_iota(jnp.int32, (rows, grads_ref.shape[0]), 0)
    pick = jnp.zeros(position.shape, f32)
    weight = jnp.zeros(position.shape, f32)
    for k, target in enumerate(targets(table, half_ref[0, 0], first, last)):
        hit = position == target
        pick = jnp.where(hit, 1.0, pick)
        weight = jnp.where(hit, gates_ref[k : k + 1, :], weight)
    gate = jnp.sum(weight, axis=1, keepdims=True)
    picked = jnp.dot(pick.astype(bf16), grads_ref[...], preferred_element_type=f32)
    return (gate * picked).astype(bf16)


def hidden_kernel(half_ref, routes_ref, hidden_ref, out_ref):
    rows = FLIGHT * (HIDDEN[1] - HIDDEN[0])
    places = targets(slot_table(routes_ref), half_ref[0, 0], *HIDDEN)
    picks = jnp.concatenate([one_hot(rows, target) for target in places], axis=1)
    entries = hidden_ref[...].reshape(picks.shape[1], hidden_ref.shape[2])
    packed = jnp.dot(picks, entries, preferred_element_type=f32).astype(bf16)
    spread(packed[: rows // 2], packed[rows // 2 :], HIDDEN[1] - HIDDEN[0], out_ref)


def grads_kernel(half_ref, routes_ref, gates_ref, grads_ref, *outs):
    table = slot_table(routes_ref)
    for number, (first, last) in enumerate((GRAD_FIRST, GRAD_LAST)):
        packed = packed_grads(table, half_ref, gates_ref, grads_ref, first, last)
        rows = packed.shape[0] // 2
        outs[2 * number][...] = packed[:rows]
        outs[2 * number + 1][...] = packed[rows:]


def block_shape(width, features):
    cuts = SPLITS[width][0]
    return jax.ShapeDtypeStruct((DESTS, cuts * 2 * width, features // cuts), bf16)


def rows_shape(width, features):
    return jax.ShapeDtypeStruct((DESTS * width, features), bf16)


def spread_kernel(width, own_ref, across_ref, out_ref):
    spread(own_ref, across_ref, width, out_ref)


def spread_rows(own, across, width):
    rows, features = own.shape
    return pl.pallas_call(
        functools.partial(spread_kernel, width),
        out_shape=block_shape(width, features),
        in_specs=[VMEM, VMEM],
        out_specs=VMEM,
        compiler_params=params(32),
        cost_estimate=pl.CostEstimate(flops=1, bytes_accessed=1, transcendentals=0),
    )(own, across)


def gather_kernel(width, in_ref, *outs):
    cuts, groups = SPLITS[width]
    block = cuts * 2 * width
    per = DESTS // groups
    lanes = in_ref.shape[2]
    source = lax.broadcasted_iota(jnp.int32, (1, per * block), 1)
    sender = lax.div(source, block)
    rest = source - sender * block
    cut_of = lax.div(rest, 2 * width)
    rest = rest - cut_of * (2 * width)
    half = lax.div(rest, width)
    place = half * (per * width) + sender * width + rest - half * width
    moves = [one_hot(2 * per * width, jnp.where(cut_of == cut, place, -1)) for cut in range(cuts)]
    for group in range(groups):
        piece = in_ref[group * per : (group + 1) * per].reshape(per * block, lanes)
        for cut, move in enumerate(moves):
            moved = jnp.dot(move, piece, preferred_element_type=f32).astype(bf16)
            there = slice(cut * lanes, (cut + 1) * lanes)
            if len(outs) == 2:
                here = slice(group * per * width, (group + 1) * per * width)
                outs[0][here, there] = moved[: per * width]
                outs[1][here, there] = moved[per * width :]
            else:
                outs[0][group * 2 * per * width : (group + 1) * 2 * per * width, there] = moved


def gathered(arrived, width, features, parts):
    rows = DESTS * width
    return pl.pallas_call(
        functools.partial(gather_kernel, width),
        out_shape=(jax.ShapeDtypeStruct((2 * rows // parts, features), bf16),) * parts,
        in_specs=[VMEM],
        out_specs=(VMEM,) * parts,
        compiler_params=params(32),
        cost_estimate=pl.CostEstimate(flops=1, bytes_accessed=1, transcendentals=0),
    )(arrived)


def thirds(value):
    high = value.astype(bf16)
    rest = value - high.astype(f32)
    middle = rest.astype(bf16)
    low = (rest - middle.astype(f32)).astype(bf16)
    return jnp.concatenate([high, middle, low], axis=0)


def added(value, rows):
    return value[:rows] + value[rows : 2 * rows] + value[2 * rows :]


def stats_kernel(norm, offset, count, more, q_ref, *refs):
    panels, rows = refs[:OWNERS], refs[OWNERS : OWNERS + count]
    before = refs[OWNERS + count : OWNERS + count + 2] if more else None
    cov_ref, out_ref, held, turned, sems = refs[-5:]
    block, tile = cov_ref.shape
    panel_rows = out_ref.shape[0]
    step = pl.program_id(0)
    quarter = q_ref[0, 0]

    def columns(away):
        return pl.ds(pl.multiple_of((quarter ^ away) * block, 128), block)

    @pl.when(step == 0)
    def _():
        copies = []
        at = 0
        for number, row in enumerate(rows):
            size = row.shape[0]
            copy = pltpu.make_async_copy(row, held.at[at : at + size, :], sems.at[number])
            copy.start()
            copies.append((copy, at, size))
            at += size
        for copy, at, size in copies:
            copy.wait()
        turned[...] = held[:, columns(0)].T

    tile_at = pl.ds(pl.multiple_of(step * tile, 128), tile)
    cov = jnp.dot(turned[...], held[:, tile_at], preferred_element_type=f32) * norm
    cov_ref[...] = cov + before[0][...] if more else cov

    @pl.when(step == pl.num_programs(0) - 1)
    def _():
        share = None
        for away in range(OWNERS):
            part = lax.dot_general(
                thirds(panels[away][:, offset : offset + block]),
                held[:, columns(away)],
                (((1,), (1,)), ((), ())),
                preferred_element_type=f32,
            )
            share = part if share is None else share + part
        product = jnp.dot(thirds(added(share, panel_rows)), held[:, columns(0)], preferred_element_type=f32)
        result = added(product, panel_rows) * norm
        out_ref[...] = result + before[1][...] if more else result


def stats(quarter, panels, offset, rows, norm, tile, before=None):
    features = rows[0].shape[1]
    block = features // OWNERS
    total = sum(row.shape[0] for row in rows)
    panel_rows, panel_width = panels[0].shape
    cov_spec = pl.BlockSpec((block, tile), lambda n: (0, n))
    out_spec = pl.BlockSpec((panel_rows, block), lambda n: (0, 0))
    more = before is not None
    return pl.pallas_call(
        functools.partial(stats_kernel, norm, offset, len(rows), more),
        grid=(features // tile,),
        out_shape=(
            pltpu.HBM((block, features), f32),
            jax.ShapeDtypeStruct((panel_rows, block), f32),
        ),
        in_specs=[SMEM]
        + [pl.BlockSpec((panel_rows, panel_width), lambda n: (0, 0))] * OWNERS
        + [HBM] * len(rows)
        + ([cov_spec, out_spec] if more else []),
        out_specs=(cov_spec, out_spec),
        scratch_shapes=[
            pltpu.VMEM((total, features), bf16),
            pltpu.VMEM((block, total), bf16),
            pltpu.SemaphoreType.DMA((len(rows),)),
        ],
        input_output_aliases={1 + OWNERS + len(rows): 0, 2 + OWNERS + len(rows): 1} if more else {},
        compiler_params=params(40),
        cost_estimate=pl.CostEstimate(flops=1, bytes_accessed=1, transcendentals=0),
    )(quarter, *panels, *rows, *(before or ()))


def core_swapped(value):
    return lax.ppermute(value, "core", [(0, 1), (1, 0)])


def y_moved(value, flip):
    return lax.ppermute(value, ("yh", "yl"), [(i, i ^ flip) for i in range(4)])


def after(value, *events):
    return lax.optimization_barrier((value, events))[0]


def along_xz(value):
    return lax.all_to_all(value, ("x", "z"), 0, 0, tiled=True)


def per_device(hidden_rows, out_grads, gates, routes, panel_a, panel_g):
    tok, slots, width_in = hidden_rows.shape
    width_out = out_grads.shape[1]
    norm = ROUTED / (tok * 256 * slots)
    routes_t = routes.T
    gates_t = gates.T
    my_half = lax.axis_index("yh").astype(jnp.int32).reshape(1, 1)
    quarter = (lax.axis_index("yl") * 2 + lax.axis_index("core")).astype(jnp.int32).reshape(1, 1)
    whole, first, last = (end - start for start, end in (HIDDEN, GRAD_FIRST, GRAD_LAST))
    sent_h = pl.pallas_call(
        hidden_kernel,
        grid=(1,),
        out_shape=block_shape(whole, width_in),
        in_specs=[
            SMEM,
            pl.BlockSpec((slots, tok), lambda n: (0, 0)),
            pl.BlockSpec((slots, tok, width_in), lambda n: (0, 0, 0)),
        ],
        out_specs=pl.BlockSpec(block_shape(whole, width_in).shape, lambda n: (0, 0, 0)),
        compiler_params=params(62),
    )(my_half, routes_t, hidden_rows.transpose(1, 0, 2))
    own_b, across_b, own_c, across_c = pl.pallas_call(
        grads_kernel,
        out_shape=(rows_shape(first, width_out),) * 2 + (rows_shape(last, width_out),) * 2,
        in_specs=[SMEM, VMEM, VMEM, VMEM],
        out_specs=(VMEM,) * 4,
        compiler_params=params(32),
    )(my_half, routes_t, gates_t, out_grads)
    panel = jnp.concatenate([panel_a[0], panel_g[0]], axis=1)
    panels = [panel] + [
        lax.ppermute(panel, ("yl", "core"), [(i, i ^ away) for i in range(OWNERS)]) for away in range(1, OWNERS)
    ]
    sent_b = spread_rows(own_b, y_moved(across_b, 3), first)
    sent_c = spread_rows(own_c, y_moved(across_c, 3), last)
    at = width_in // OWNERS

    got_h = along_xz(sent_h)
    got_h, sent_b, sent_c, panels = lax.optimization_barrier((got_h, sent_b, sent_c, panels))
    got_b = along_xz(sent_b)
    own_h, across_h = gathered(got_h, whole, width_in, 2)
    beside_h, crossed_h = y_moved(own_h, 1), y_moved(across_h, 3)
    relayed_h = y_moved(crossed_h, 1)
    got_b = after(got_b, beside_h, relayed_h)
    sent_c = after(sent_c, got_b)
    rows_h = [own_h, beside_h, crossed_h, relayed_h]
    rows_h = rows_h + [core_swapped(piece) for piece in rows_h]
    (own_b,) = gathered(got_b, first, width_out, 1)
    beside_b = y_moved(own_b, 1)
    got_c = along_xz(sent_c)
    input_cov, input_panel = stats(quarter, panels, 0, after(rows_h, own_b), norm, 768)
    rows_b = after([own_b, core_swapped(own_b)], input_cov)
    begun_g = stats(quarter, panels, at, rows_b, norm, 1280)
    swapped_b = core_swapped(after(beside_b, begun_g))
    (own_c,) = gathered(after(got_c, begun_g), last, width_out, 1)
    beside_c = y_moved(own_c, 1)
    rows_d = after([beside_b, swapped_b, own_c, core_swapped(own_c)], own_c)
    going_g = stats(quarter, panels, at, rows_d, norm, 1280, begun_g)
    beside_c = after(beside_c, going_g)
    grad_cov, grad_panel = stats(quarter, panels, at, [beside_c, core_swapped(beside_c)], norm, 1280, going_g)
    return (input_cov[None], grad_cov[None], input_panel[None], grad_panel[None])


def solution(mesh):
    split = Mesh(mesh.devices.reshape(4, 2, 2, 2, Z), AXES)
    return jax.shard_map(
        per_device,
        mesh=split,
        in_specs=(
            P(AXES, None, None),
            P(AXES, None),
            P(AXES, None),
            P(AXES, None),
            P(AXES, None, None),
            P(AXES, None, None),
        ),
        out_specs=(P(AXES, None, None),) * 4,
        check_vma=False,
    )
```
